512 devices in a mesh: tm: 4 (over z_lo, core), height: 16 (over x, z_hi), group: 8 (over y).
Axes of the slice: x: 4, y: 8, z: 8 (z_hi: 4, z_lo: 2; z = z_hi * 2 + z_lo), core: 2. Of those that a mesh axis runs over, the one named last changes fastest.
Arguments:
- queries: bfloat16 [8, 8, 32, 32, 1536], P('group', 'tm', 'height'), may hold values from -5 to 5
- keys: bfloat16 [8, 8, 32, 32, 1536], P('group', 'tm', 'height'), may hold values from -5 to 5
- values: bfloat16 [8, 8, 32, 32, 1536], P('group', 'tm', 'height'), may hold values from -6 to 6
- window: int32 [12, 3], replicated, may hold values from 0 to 2, as said below
- adapter_down_factor: bfloat16 [1536, 64], P('height'), may hold values from -0.15625 to 0.15625
- adapter_up_factor: bfloat16 [64, 3072], P(None, 'height'), may hold values from -0.75 to 0.75
- stream: bfloat16 [8, 8, 32, 32, 3072], P('group', 'tm', 'height'), may hold values from -6 to 6
- modulation: float32 [8, 3, 3072], P('group'), may hold values from -3 to 3
- closing_weight: bfloat16 [3072, 64], replicated, may hold values from -0.109375 to 0.109375
- closing_bias: float32 [64], replicated, may hold values from -3 to 3
- latent: float32 [8, 8, 32, 2048], P('group', 'tm', 'height'), may hold values from -6 to 6
- next_latent_sample: float32 [8, 8, 32, 2048], P('group', 'tm', 'height'), may hold values from -12.5 to 12.5
- sampling_log_probability: float32 [8], P('group'), may hold values from -5 to -2, as said below
- advantage: float32 [8], P('group'), may hold values from -2 to 2, as said below
Outputs:
- gradient_down_factor: float32 [1536, 64], P('height')
- gradient_up_factor: float32 [64, 3072], P(None, 'height')
The draws below stay inside these ranges and needn't reach their ends.
Inputs may be any that keep to these rules, and one draw needn't show every extreme that they name: `window`: every head reaches at most 1 frame, 1 row and 2 tiles either way; in every draw some head reaches 1 frame, some head 1 row and some head 2 tiles. `sampling_log_probability`: each value lies in -2.9 to -2.0 or in -5.0 to -4.1. A rollout's advantage is positive, 0.5 to 2, where its sampling log-probability is -2.9 or more, and negative, -2 to -0.5, where it is -4.1 or less.
All inputs are finite; a program needn't handle non-finite values.
Results may differ from the reference program's by a relative error of at most 0.01.
Values may be sent and summed in bfloat16 or wider, within the bound.
A program may use at most 64 MiB of HBM per device.

```python
import math
import jax
import jax.numpy as jnp
from jax import lax

COLS = 32
TILE_W = 8
LOCAL_HEADS = 12
HEAD_WIDTH = 128
MODEL_DIMENSION = 3072
ADAPTER_RANK = 64
LAT = 64
FRAMES = 8
ROWS = 32
ROLLOUTS = 8


def rollout_bands(key):
    side_key, place_key, size_key = jax.random.split(jax.random.fold_in(key, 29), 3)
    upper_side = jax.random.bernoulli(side_key, 0.5, (ROLLOUTS,))
    place = jax.random.uniform(place_key, (ROLLOUTS,), jnp.float32, 0.0, 0.9)
    magnitude = jax.random.uniform(size_key, (ROLLOUTS,), jnp.float32, 0.5, 2.0)
    return (upper_side, place, magnitude)


def draw_queries(key, part):
    key = jax.random.fold_in(key, 11)
    full_shape = (ROLLOUTS, FRAMES, ROWS, COLS, LOCAL_HEADS * HEAD_WIDTH)
    drawn_field = jnp.clip(jax.random.normal(key, full_shape, jnp.float32), -4.5, 4.5)
    return drawn_field.astype(jnp.bfloat16)


def draw_keys(key, part):
    key = jax.random.fold_in(key, 13)
    full_shape = (ROLLOUTS, FRAMES, ROWS, COLS, LOCAL_HEADS * HEAD_WIDTH)
    drawn_field = jnp.clip(jax.random.normal(key, full_shape, jnp.float32), -4.5, 4.5)
    return drawn_field.astype(jnp.bfloat16)


def draw_window(key, part):
    key = jax.random.fold_in(key, 5)
    first, second, third, fourth = jax.random.split(key, 4)
    window_reach = jnp.stack([jax.random.randint(first, (LOCAL_HEADS,), 0, 2), jax.random.randint(second, (LOCAL_HEADS,), 0, 2), jax.random.randint(third, (LOCAL_HEADS,), 0, 3)], axis=1).astype(jnp.int32)
    chosen_heads = jax.random.randint(fourth, (3,), 0, LOCAL_HEADS).astype(jnp.int32)
    highest = jnp.array([1, 1, 2], jnp.int32)
    head_iota = jnp.arange(LOCAL_HEADS, dtype=jnp.int32)[:, None]
    return jnp.where(head_iota == chosen_heads[None, :], highest[None, :], window_reach).astype(jnp.int32)


def draw_next_latent_sample(key, part):
    key = jax.random.fold_in(key, 7)
    full_shape = (ROLLOUTS, FRAMES, ROWS, COLS * LAT)
    frame_at = lax.broadcasted_iota(jnp.int32, full_shape, 1).astype(jnp.float32)
    row_at = lax.broadcasted_iota(jnp.int32, full_shape, 2).astype(jnp.float32)
    scale_ramp = (1.0 + 0.75 * frame_at / (FRAMES - 1)) * (1.0 + 0.75 * row_at / (ROWS - 1))
    drawn_field = jnp.clip(jax.random.normal(key, full_shape, jnp.float32), -4.0, 4.0)
    return (drawn_field * scale_ramp).astype(jnp.float32)


def draw_sampling_log_probability(key, part):
    upper_side, place, magnitude = rollout_bands(key)
    return jnp.where(upper_side, -2.9 + place, -5.0 + place).astype(jnp.float32)


def draw_advantage(key, part):
    upper_side, place, magnitude = rollout_bands(key)
    return jnp.where(upper_side, magnitude, -magnitude).astype(jnp.float32)


def block_levels(stream_key, extent, pieces, least, largest):
    level = 1.0
    for axis_at, blocks in pieces:
        draws = jax.random.uniform(jax.random.fold_in(jax.random.fold_in(stream_key, 6), axis_at), (blocks,), jnp.float32, least / len(pieces), largest / len(pieces))
        level = level * jnp.repeat(jnp.exp(draws), extent[axis_at] // blocks).reshape((-1,) + (1,) * (len(extent) - 1 - axis_at))
    return level


def gaussian(rng, extent, scale, limit, cuts=(), kind=jnp.bfloat16):
    values = jax.random.normal(rng, extent, jnp.float32) * scale
    if len(cuts) > 0:
        values = block_levels(rng, extent, cuts, -0.22, 0.18) * values
    return jnp.clip(values, min=-limit, max=limit).astype(kind)


def setup_inputs(seed: int = 0) -> dict:
    seeds = jax.random.split(jax.random.key(seed), 15)
    queries = draw_queries(jax.random.fold_in(seeds[14], 71), 0)
    keys = draw_keys(jax.random.fold_in(seeds[14], 71), 0)
    values = gaussian(seeds[2], (ROLLOUTS, FRAMES, ROWS, COLS, LOCAL_HEADS * HEAD_WIDTH), 1.0, 6.0, ((0, 8), (1, 4), (2, 16)))
    window = draw_window(jax.random.fold_in(seeds[14], 71), 0)
    adapter_down_factor = gaussian(seeds[4], (LOCAL_HEADS * HEAD_WIDTH, ADAPTER_RANK), (LOCAL_HEADS * HEAD_WIDTH) ** -0.5, 0.15625, ((0, 16),))
    adapter_up_factor = gaussian(seeds[5], (ADAPTER_RANK, MODEL_DIMENSION), ADAPTER_RANK ** -0.5, 0.75, ((1, 16),))
    stream = gaussian(seeds[6], (ROLLOUTS, FRAMES, ROWS, COLS, MODEL_DIMENSION), 1.0, 6.0, ((0, 8), (1, 4), (2, 16)))
    modulation = gaussian(seeds[7], (ROLLOUTS, 3, MODEL_DIMENSION), 0.5, 3.0, ((0, 8),), jnp.float32)
    closing_weight = gaussian(seeds[8], (MODEL_DIMENSION, LAT), MODEL_DIMENSION ** -0.5, 0.109375)
    closing_bias = gaussian(seeds[9], (LAT,), 0.5, 3.0, (), jnp.float32)
    latent = gaussian(seeds[10], (ROLLOUTS, FRAMES, ROWS, COLS * LAT), 1.0, 6.0, ((0, 8), (1, 4), (2, 16)), jnp.float32)
    next_latent_sample = draw_next_latent_sample(jax.random.fold_in(seeds[14], 71), 0)
    sampling_log_probability = draw_sampling_log_probability(jax.random.fold_in(seeds[14], 71), 0)
    advantage = draw_advantage(jax.random.fold_in(seeds[14], 71), 0)
    return {"queries": queries, "keys": keys, "values": values, "window": window, "adapter_down_factor": adapter_down_factor, "adapter_up_factor": adapter_up_factor, "stream": stream, "modulation": modulation, "closing_weight": closing_weight, "closing_bias": closing_bias, "latent": latent, "next_latent_sample": next_latent_sample, "sampling_log_probability": sampling_log_probability, "advantage": advantage}


SAMPLER_STEP = -0.5
CLIP_RANGE = 0.2
NORM_EPS = 1e-06
HALF_LOG_TAU = 0.5 * math.log(2.0 * math.pi)

def tile_mask(window, gap_frame, gap_row, gap_tile, inside):
    return (gap_frame[None] <= window[:, 0][:, None, None]) & (gap_row[None] <= window[:, 1][:, None, None]) & (gap_tile[None] <= window[:, 2][:, None, None]) & inside[None, None, :]

def attend(query_block, key_block, value_block, allowed):
    scale = query_block.shape[-1] ** (-0.5)
    scores = jnp.einsum('qhd,khd->hqk', query_block.astype(jnp.float32), key_block.astype(jnp.float32)) * scale
    scores = jnp.where(allowed, scores, -1e+30)
    row_max = lax.optimization_barrier(jnp.max(scores, axis=-1, keepdims=True))
    expo_terms = jnp.where(allowed, jnp.exp(scores - row_max), 0.0)
    row_sum = lax.optimization_barrier(jnp.sum(expo_terms, axis=-1, keepdims=True))
    weights = lax.optimization_barrier((expo_terms / row_sum).astype(jnp.bfloat16))
    mixed = jnp.einsum('hqk,khd->qhd', weights.astype(jnp.float32), value_block.astype(jnp.float32))
    return mixed.astype(jnp.bfloat16)

def head_forward_pass(attention_result, flowing_rows, modulation, adapter_down_factor, adapter_up_factor, closing_weight, closing_bias):
    lowrank_update = jnp.dot(attention_result, adapter_down_factor, preferred_element_type=jnp.float32).astype(jnp.bfloat16)
    adapter_result = jnp.dot(lowrank_update, adapter_up_factor, preferred_element_type=jnp.float32)
    hidden = flowing_rows.astype(jnp.float32) + modulation[0] * adapter_result
    centre = lax.optimization_barrier(jnp.mean(hidden, axis=-1, keepdims=True))
    spread = lax.optimization_barrier(jnp.mean((hidden - centre) ** 2, axis=-1, keepdims=True))
    inverse_deviation = lax.rsqrt(spread + NORM_EPS)
    normalized_rows = (hidden - centre) * inverse_deviation
    normed = (normalized_rows * (1.0 + modulation[2]) + modulation[1]).astype(jnp.bfloat16)
    predicted_velocity = jnp.dot(normed, closing_weight, preferred_element_type=jnp.float32) + closing_bias
    return (lowrank_update, normalized_rows, inverse_deviation, predicted_velocity)

def reverse_pass(residual_rows, lowrank_update, normalized_rows, inverse_deviation, attention_result, modulation, adapter_up_factor, closing_weight):
    upper_part = lax.Precision.HIGHEST
    g_velocity = SAMPLER_STEP * residual_rows
    g_normed = jnp.dot(g_velocity, closing_weight.astype(jnp.float32).T, precision=upper_part)
    g_normal = g_normed * (1.0 + modulation[2])
    g_hidden = inverse_deviation * (g_normal - lax.optimization_barrier(jnp.mean(g_normal, axis=-1, keepdims=True)) - normalized_rows * lax.optimization_barrier(jnp.mean(g_normal * normalized_rows, axis=-1, keepdims=True)))
    gradient_output = modulation[0] * g_hidden
    low_wide = lax.optimization_barrier(lowrank_update).astype(jnp.float32)
    attended_wide = lax.optimization_barrier(attention_result).astype(jnp.float32)
    gradient_up_factor = jnp.dot(low_wide.T, gradient_output, precision=upper_part)
    gradient_lowrank = jnp.dot(gradient_output, adapter_up_factor.astype(jnp.float32).T, precision=upper_part)
    gradient_down_factor = jnp.dot(attended_wide.T, gradient_lowrank, precision=upper_part)
    return (gradient_down_factor, gradient_up_factor)

def slopes(log_prob, sampling_log_probability, advantage, count):

    def surrogate(value):
        ratio = jnp.exp(value - sampling_log_probability)
        return jnp.maximum(-advantage * ratio, -advantage * jnp.clip(ratio, 1.0 - CLIP_RANGE, 1.0 + CLIP_RANGE))
    _, pull = jax.vjp(surrogate, log_prob)
    return pull(jnp.ones_like(log_prob) / count)[0]

def reference(queries, keys, values, window, adapter_down_factor, adapter_up_factor, stream, modulation, closing_weight, closing_bias, latent, next_latent_sample, sampling_log_probability, advantage):
    rollouts, frames, row_count, col_count, feature_width = queries.shape
    head_count = window.shape[0]
    head_size = feature_width // head_count
    lat_width = closing_weight.shape[1]
    padding = ((0, 0), (1, 1), (1, 1), (0, 0), (0, 0))
    key_pad = jnp.pad(keys, padding)
    value_pad = jnp.pad(values, padding)
    three_span = jnp.arange(3, dtype=jnp.int32)
    key_frame, key_row, key_col = jnp.meshgrid(three_span, three_span, jnp.arange(col_count, dtype=jnp.int32), indexing='ij')
    key_frame = key_frame.ravel()
    key_row = key_row.ravel()
    key_col = key_col.ravel()
    key_total = key_frame.shape[0]
    query_col = jnp.arange(col_count, dtype=jnp.int32)
    gap_frame = jnp.broadcast_to(jnp.abs(key_frame - 1)[None, :], (col_count, key_total))
    gap_row = jnp.broadcast_to(jnp.abs(key_row - 1)[None, :], (col_count, key_total))
    gap_tile = jnp.abs(query_col[:, None] // TILE_W - key_col[None, :] // TILE_W)
    zero_index = jnp.zeros((), jnp.int32)

    def block(block_index):
        rollout_trajectory = (block_index // (frames * row_count)).astype(jnp.int32)
        frame_at = (block_index // row_count % frames).astype(jnp.int32)
        row_at = (block_index % row_count).astype(jnp.int32)
        start = (rollout_trajectory, frame_at, row_at, zero_index, zero_index)
        query_block = lax.dynamic_slice(queries, start, (1, 1, 1, col_count, feature_width)).reshape(col_count, head_count, head_size)
        key_block = lax.dynamic_slice(key_pad, start, (1, 3, 3, col_count, feature_width)).reshape(key_total, head_count, head_size)
        value_block = lax.dynamic_slice(value_pad, start, (1, 3, 3, col_count, feature_width)).reshape(key_total, head_count, head_size)
        frame_global = frame_at - 1 + key_frame
        row_global = row_at - 1 + key_row
        inside = (frame_global >= 0) & (frame_global < frames) & (row_global >= 0) & (row_global < row_count)
        allowed = tile_mask(window, gap_frame, gap_row, gap_tile, inside)
        return attend(query_block, key_block, value_block, allowed).reshape(col_count, feature_width)
    attention_result = lax.map(block, jnp.arange(rollouts * frames * row_count, dtype=jnp.int32))
    attention_result = attention_result.reshape(rollouts, frames * row_count * col_count, feature_width)
    width_of_model = stream.shape[-1]
    count = frames * row_count * col_count * lat_width

    def rollout_state(rollout_trajectory):
        lowrank_update, normalized_rows, inverse_deviation, predicted_velocity = head_forward_pass(attention_result[rollout_trajectory], stream[rollout_trajectory].reshape(-1, width_of_model), modulation[rollout_trajectory], adapter_down_factor, adapter_up_factor, closing_weight, closing_bias)
        mean_next = latent[rollout_trajectory] + SAMPLER_STEP * predicted_velocity.reshape(frames, row_count, col_count * lat_width)
        residue = next_latent_sample[rollout_trajectory] - mean_next
        return (lowrank_update, normalized_rows, inverse_deviation, residue)

    def fit(rollout_trajectory):
        residue = rollout_state(rollout_trajectory)[3]
        return jnp.sum(residue * residue)
    partials = lax.map(fit, jnp.arange(rollouts, dtype=jnp.int32))
    log_prob = -partials / (2.0 * count) - HALF_LOG_TAU
    slope_all = slopes(log_prob, sampling_log_probability, advantage, rollouts)

    def accumulate(running, rollout_trajectory):
        lowrank_update, normalized_rows, inverse_deviation, residue = rollout_state(rollout_trajectory)
        residual_rows = (slope_all[rollout_trajectory] * residue).reshape(-1, lat_width)
        gradient_down_factor, gradient_up_factor = reverse_pass(residual_rows, lowrank_update, normalized_rows, inverse_deviation, attention_result[rollout_trajectory], modulation[rollout_trajectory], adapter_up_factor, closing_weight)
        return ((running[0] + gradient_down_factor, running[1] + gradient_up_factor), None)
    initial_sums = (jnp.zeros(adapter_down_factor.shape, jnp.float32), jnp.zeros(adapter_up_factor.shape, jnp.float32))
    (gradient_down_factor, gradient_up_factor), _ = lax.scan(accumulate, initial_sums, jnp.arange(rollouts, dtype=jnp.int32))
    return (gradient_down_factor, gradient_up_factor)
```

```python
import functools
import math

import jax
import jax.numpy as jnp
from jax import lax
from jax.experimental import pallas as pl
from jax.experimental.pallas import tpu as pltpu
from jax.sharding import PartitionSpec as P

TILE_W = 8
COLS = 32
HEAD = 128
RANK = 64
LAT = 64
SAMPLER_STEP = -0.5
CLIP_RANGE = 0.2
NORM_EPS = 1e-06
HALF_LOG_TAU = 0.5 * math.log(2.0 * math.pi)
DOWN_SHARD = 96
UP_SHARD = 192
PIECE = 144
HALF = 80
FAR = 32768.0
F32 = jnp.float32
BF16 = jnp.bfloat16
MESH = pl.DeviceIdType.MESH


def dot(a, b, ca, cb):
    return lax.dot_general(a, b, (((ca,), (cb,)), ((), ())), preferred_element_type=F32)


def kernel(
    dims,
    q_hbm, k_hbm, v_hbm, win, a_t, b_own, st_hbm, mod, w_hbm, bias, lat, nxt, slp, adv,
    out,
    q, kv, st, w_t, gath, a_full, b_full, att, hid, gn, pack, mate, chip, got, ysum, final,
    d2, dn, part_tm, part_h, load_sem, halo_send, halo_recv, g_send, g_recv, s_send, s_recv,
    r_send, r_recv,
):
    n_tm, n_h, n_g, n_z, heads, group_heads = dims
    width = heads * HEAD
    model = st.shape[-1]
    n_x = n_h // n_z
    tm, me_h, me_g = lax.axis_index("tm"), lax.axis_index("height"), lax.axis_index("group")
    core, z_lo = lax.rem(tm, 2), tm // 2
    me_x, me_z = me_h // n_z, lax.rem(me_h, n_z)
    half_h = n_h // 2

    loads = [
        pltpu.make_async_copy(k_hbm.at[0], kv.at[0, 1:3, 1:3], load_sem.at[0]),
        pltpu.make_async_copy(v_hbm.at[0], kv.at[1, 1:3, 1:3], load_sem.at[1]),
        pltpu.make_async_copy(q_hbm.at[0], q, load_sem.at[2]),
        pltpu.make_async_copy(st_hbm.at[0], st, load_sem.at[3]),
        pltpu.make_async_copy(w_hbm, w_t, load_sem.at[4]),
    ]
    for load in loads:
        load.start()

    barrier = pltpu.get_barrier_semaphore()
    plane = 2 * n_h

    def greet_plane(i, _):
        at = lax.rem(me_h * 2 + z_lo + i, plane)
        pl.semaphore_signal(
            barrier, inc=1, device_id=(2 * lax.rem(at, 2) + core, at // 2, me_g), device_id_type=MESH
        )
        return 0

    lax.fori_loop(1, plane, greet_plane, 0)

    def greet_group(i, _):
        pl.semaphore_signal(
            barrier, inc=1, device_id=(tm, me_h, lax.rem(me_g + i, n_g)), device_id_type=MESH
        )
        return 0

    lax.fori_loop(1, n_g, greet_group, 0)
    for zl in range(2):
        pl.semaphore_signal(
            barrier, inc=1, device_id=(2 * zl + 1 - core, me_h, me_g), device_id_type=MESH
        )

    lane = lax.broadcasted_iota(jnp.int32, (1, 128), 1)
    left = lane < 64
    unit_row = lax.broadcasted_iota(jnp.int32, (64, 128), 0)
    unit_lane = lax.broadcasted_iota(jnp.int32, (64, 128), 1)
    twice = (lax.rem(unit_lane, 64) == unit_row).astype(F32).astype(BF16)
    b_rows = dot(b_own[...], twice, 0, 0)
    a_rows = dot(a_t[...], twice, 0, 0)
    own_rows = jnp.concatenate(
        [jnp.where(left, b_rows[0:96], b_rows[96:192]), jnp.where(left, a_rows[0:48], a_rows[48:96])],
        axis=0,
    ).astype(BF16)

    @pl.when(core == 0)
    def _():
        gath[me_h, 0:HALF, :] = own_rows[0:HALF]

    @pl.when(core == 1)
    def _():
        gath[me_h, HALF:PIECE, :] = own_rows[HALF:PIECE]

    first_tm, last_tm = tm == 0, tm == n_tm - 1
    first_h, last_h = me_h == 0, me_h == n_h - 1

    @pl.when(first_tm)
    def _():
        kv[:, 0:1] = jnp.zeros((2, 1, 4, COLS, width), BF16)

    @pl.when(last_tm)
    def _():
        kv[:, 3:4] = jnp.zeros((2, 1, 4, COLS, width), BF16)

    @pl.when(first_h)
    def _():
        kv[:, :, 0:1] = jnp.zeros((2, 4, 1, COLS, width), BF16)

    @pl.when(last_h)
    def _():
        kv[:, :, 3:4] = jnp.zeros((2, 4, 1, COLS, width), BF16)

    loads[0].wait()
    loads[1].wait()
    pl.semaphore_wait(barrier, plane - 1 + n_g - 1 + 2)

    n_parts = heads // group_heads
    ahead_h = (tm, jnp.minimum(me_h + 1, n_h - 1), me_g)
    back_h = (tm, jnp.maximum(me_h - 1, 0), me_g)
    ahead_tm = (jnp.minimum(tm + 1, n_tm - 1), me_h, me_g)
    back_tm = (jnp.maximum(tm - 1, 0), me_h, me_g)

    def halo(part, way):
        cols = pl.ds(part * group_heads * HEAD, group_heads * HEAD)
        src, dst, to = {
            0: (kv.at[:, 1:3, 2, :, cols], kv.at[:, 1:3, 0, :, cols], ahead_h),
            1: (kv.at[:, 1:3, 1, :, cols], kv.at[:, 1:3, 3, :, cols], back_h),
            2: (kv.at[:, 2, 1:3, :, cols], kv.at[:, 0, 1:3, :, cols], ahead_tm),
            3: (kv.at[:, 1, 1:3, :, cols], kv.at[:, 3, 1:3, :, cols], back_tm),
            4: (kv.at[:, 2, 0, :, cols], kv.at[:, 0, 0, :, cols], ahead_tm),
            5: (kv.at[:, 1, 0, :, cols], kv.at[:, 3, 0, :, cols], back_tm),
            6: (kv.at[:, 2, 3, :, cols], kv.at[:, 0, 3, :, cols], ahead_tm),
            7: (kv.at[:, 1, 3, :, cols], kv.at[:, 3, 3, :, cols], back_tm),
        }[way]
        return pltpu.make_async_remote_copy(
            src_ref=src, dst_ref=dst, send_sem=halo_send.at[part, way], recv_sem=halo_recv.at[part, way],
            device_id=to, device_id_type=MESH,
        )

    not_first_tm, not_last_tm = tm > 0, tm < n_tm - 1
    not_first_h, not_last_h = me_h > 0, me_h < n_h - 1
    sends = {
        0: not_last_h, 1: not_first_h, 2: not_last_tm, 3: not_first_tm,
        4: not_first_h & not_last_tm, 5: not_first_h & not_first_tm,
        6: not_last_h & not_last_tm, 7: not_last_h & not_first_tm,
    }
    receives = {
        0: not_first_h, 1: not_last_h, 2: not_first_tm, 3: not_last_tm,
        4: not_first_h & not_first_tm, 5: not_first_h & not_last_tm,
        6: not_last_h & not_first_tm, 7: not_last_h & not_last_tm,
    }

    def when_each(table, ways, part, act):
        for way in ways:
            @pl.when(table[way])
            def _(way=way):
                act(halo(part, way))

    my_rows = pl.ds(pl.multiple_of(core * HALF, 16), HALF)

    def gather_z(i):
        src = gath.at[me_h, my_rows]
        to = (tm, me_x * n_z + lax.rem(me_z + i, n_z), me_g)
        return pltpu.make_async_remote_copy(
            src_ref=src, dst_ref=src, send_sem=g_send.at[i], recv_sem=g_recv.at[0],
            device_id=to, device_id_type=MESH,
        )

    def gather_x(i):
        src = gath.at[pl.ds(me_x * n_z, n_z), my_rows]
        to = (tm, lax.rem(me_x + i, n_x) * n_z + me_z, me_g)
        return pltpu.make_async_remote_copy(
            src_ref=src, dst_ref=src, send_sem=g_send.at[n_z + i], recv_sem=g_recv.at[1],
            device_id=to, device_id_type=MESH,
        )

    def gather_core():
        src = gath.at[:, my_rows]
        return pltpu.make_async_remote_copy(
            src_ref=src, dst_ref=src, send_sem=g_send.at[0], recv_sem=g_recv.at[2],
            device_id=(2 * z_lo + 1 - core, me_h, me_g), device_id_type=MESH,
        )

    for part in range(n_parts):
        when_each(sends, (0, 1, 2, 3), part, lambda copy: copy.start())
        if part == 0:
            for i in range(1, n_z):
                gather_z(i).start()

    tokens = 4 * COLS
    q_at = lax.broadcasted_iota(jnp.int32, (tokens, 128), 0)
    feature = lax.broadcasted_iota(jnp.int32, (tokens, 128), 1)
    q_frame, q_row, q_tile = q_at // 64, lax.rem(q_at // 32, 2), lax.rem(q_at, 32) // TILE_W
    frame_at = tm * 2 - 1 + feature
    row_at = me_h * 2 - 1 + (feature - 4)
    gap_frame = jnp.where(
        (frame_at >= 0) & (frame_at < 2 * n_tm), jnp.abs(q_frame + 1 - feature), 99
    )
    gap_row = jnp.where(
        (row_at >= 0) & (row_at < 2 * n_h), jnp.abs(q_row + 1 - (feature - 4)), 99
    )
    gap_tile = jnp.abs(q_tile - (feature - 8))
    gap = jnp.where(
        feature < 4, gap_frame,
        jnp.where(feature < 8, gap_row, jnp.where(feature < 12, gap_tile, -1)),
    )
    k_at = lax.broadcasted_iota(jnp.int32, (512, 128), 0)
    k_feature = lax.broadcasted_iota(jnp.int32, (512, 128), 1)
    k_one_hot = (
        (k_feature == k_at // 128)
        | (k_feature == 4 + lax.rem(k_at // 32, 4))
        | (k_feature == 8 + lax.rem(k_at, 32) // TILE_W)
    ).astype(F32).astype(BF16)
    ones = jnp.ones((512, 128), BF16)
    factor = HEAD**-0.5 * math.log2(math.e)

    def attend(part):
        for head in range(part * group_heads, (part + 1) * group_heads):
            cols = pl.ds(head * HEAD, HEAD)
            reach = jnp.where(
                lane < 4, win[0, head], jnp.where(lane < 8, win[1, head], win[2, head])
            )
            penalty = jnp.where(gap > reach, -FAR, 0.0).astype(BF16)
            query = jnp.concatenate([q[:, :, :, cols].reshape(tokens, HEAD), penalty], axis=1)
            key = jnp.concatenate([kv[0, :, :, :, cols].reshape(512, HEAD), k_one_hot], axis=1)
            scores = dot(query, key, 1, 1)
            top = jnp.max(scores, axis=1, keepdims=True)
            terms = jnp.exp2((scores - top) * factor).astype(BF16)
            value = jnp.concatenate([kv[1, :, :, :, cols].reshape(512, HEAD), ones], axis=1)
            mixed = dot(terms, value, 1, 0)
            att[:, cols] = (mixed[:, :HEAD] / mixed[:, HEAD:]).astype(BF16)

    loads[2].wait()
    for part in range(n_parts):
        when_each(receives, (0, 1), part, lambda copy: copy.wait_recv())
        when_each(sends, (4, 5, 6, 7), part, lambda copy: copy.start())
        if part == 0:
            for i in range(1, n_z):
                gather_z(i).wait_send()
            taken = gath.at[pl.ds(0, n_z - 1), my_rows]
            pltpu.make_async_copy(taken, taken, g_recv.at[0]).wait()
            for i in range(1, n_x):
                gather_x(i).start()
        if part == 1:
            for i in range(1, n_x):
                gather_x(i).wait_send()
            taken = gath.at[pl.ds(0, (n_x - 1) * n_z), my_rows]
            pltpu.make_async_copy(taken, taken, g_recv.at[1]).wait()
            gather_core().start()
        if part >= 1:
            when_each(receives, (2, 3, 4, 5, 6, 7), part - 1, lambda copy: copy.wait_recv())
            attend(part - 1)
        if part == min(2, n_parts - 1):
            gather_core().wait()
            for h in range(n_h):
                both = gath[h, 0:96, :]
                b_full[h * 192 : h * 192 + 96, :] = both
                b_full[h * 192 + 96 : h * 192 + 192, 0:64] = both[:, 64:128]
                both = gath[h, 96:144, :]
                a_full[h * 96 : h * 96 + 48, :] = both
                a_full[h * 96 + 48 : h * 96 + 96, 0:64] = both[:, 64:128]
            for f in range(2):
                for j in range(16):
                    cols = pl.ds(j * 128, 128)
                    d2[pl.ds(f * 32 + 2 * j, 2), :] = nxt[0, f, :, cols] - lat[0, f, :, cols]
            for f in range(2):
                for r in range(2):
                    pair = d2[pl.ds(f * 32 + r, 16, stride=2), :]
                    dn[pl.ds(f * 64 + r * 32, 16, stride=2), :] = pair
                    dn[pl.ds(f * 64 + r * 32 + 1, 16, stride=2), :] = pltpu.roll(pair, 64, 1)
            loads[3].wait()
            loads[4].wait()
    when_each(receives, (2, 3, 4, 5, 6, 7), n_parts - 1, lambda copy: copy.wait_recv())
    attend(n_parts - 1)

    step = 2 * UP_SHARD
    chunks = [pl.ds(i * step, step) for i in range(model // step)]

    def fold(x):
        total = x[:, 0:128]
        for i in range(1, x.shape[1] // 128):
            total = total + x[:, i * 128 : (i + 1) * 128]
        return total

    def mean(total):
        return jnp.sum(total, axis=1, keepdims=True) * (1.0 / model)

    low = dot(att[...], a_full[:, 0:64], 1, 0).astype(BF16)
    total = jnp.zeros((tokens, 128), F32)
    for cols in chunks:
        update = dot(low, b_full[cols, 0:64], 1, 1)
        rows = st[:, :, :, cols].reshape(tokens, step).astype(F32)
        hidden = rows + mod[0, :, cols] * update
        hid[:, cols] = hidden
        total = total + fold(hidden)
    centre = mean(total)
    total = jnp.zeros((tokens, 128), F32)
    for cols in chunks:
        apart = hid[:, cols] - centre
        total = total + fold(apart * apart)
    inverse = lax.rsqrt(mean(total) + NORM_EPS)
    velocity = jnp.zeros((tokens, LAT), F32)
    for cols in chunks:
        normal = (hid[:, cols] - centre) * inverse
        hid[:, cols] = normal
        normed = (normal * (1.0 + mod[2, :, cols]) + mod[1, :, cols]).astype(BF16)
        velocity = velocity + dot(normed, w_t[:, cols], 1, 1)
    residue = dn[:, 0:64] - SAMPLER_STEP * (velocity + bias[...])

    square = jnp.sum(jnp.sum(residue * residue, axis=0, keepdims=True), axis=1, keepdims=True)
    part_tm[tm] = jnp.broadcast_to(square, (8, 128))

    def sum_tm(i):
        return pltpu.make_async_remote_copy(
            src_ref=part_tm.at[tm], dst_ref=part_tm.at[tm], send_sem=s_send.at[i], recv_sem=s_recv.at[0],
            device_id=(lax.rem(tm + i, n_tm), me_h, me_g), device_id_type=MESH,
        )

    def sum_h(i):
        return pltpu.make_async_remote_copy(
            src_ref=part_h.at[me_h], dst_ref=part_h.at[me_h], send_sem=s_send.at[n_tm + i], recv_sem=s_recv.at[1],
            device_id=(tm, lax.rem(me_h + i, n_h), me_g), device_id_type=MESH,
        )

    for i in range(1, n_tm):
        sum_tm(i).start()

    g_velocity = (SAMPLER_STEP * residue).astype(BF16)
    total = jnp.zeros((tokens, 128), F32)
    total_n = jnp.zeros((tokens, 128), F32)
    for cols in chunks:
        g_normal = dot(g_velocity, w_t[:, cols], 1, 0) * (1.0 + mod[2, :, cols])
        gn[:, cols] = g_normal
        total = total + fold(g_normal)
        total_n = total_n + fold(g_normal * hid[:, cols])
    mean_g, mean_gn = mean(total), mean(total_n)

    for i in range(1, n_tm):
        sum_tm(i).wait_send()
    pltpu.make_async_copy(part_tm.at[0 : n_tm - 1], part_tm.at[0 : n_tm - 1], s_recv.at[0]).wait()
    square = part_tm[0]
    for i in range(1, n_tm):
        square = square + part_tm[i]
    part_h[me_h] = square
    for i in range(1, n_h):
        sum_h(i).start()

    g_low = jnp.zeros((tokens, RANK), F32)
    for pair, cols in enumerate(chunks):
        g_out = mod[0, :, cols] * (inverse * (gn[:, cols] - mean_g - hid[:, cols] * mean_gn))
        g_out = g_out.astype(BF16)
        g_low = g_low + dot(g_out, b_full[cols, 0:64], 1, 0)
        up = dot(low, g_out, 0, 0)
        pack[pair, 0, 0:64, :] = up[:, 0:128].astype(BF16)
        pack[pair, 1, 0:64, :] = up[:, 256:384].astype(BF16)
        shared = up[:, 128:256]
        turned = pltpu.roll(shared, 64, 1)
        pack[pair, 0, 64:96, :] = jnp.where(left, shared[0:32], turned[32:64]).astype(BF16)
        pack[pair, 1, 64:96, :] = jnp.where(left, turned[0:32], shared[32:64]).astype(BF16)

    partner = (2 * z_lo + 1 - core, me_h, me_g)

    def to_mate(i):
        rows = (pl.ds(0, 96), pl.ds(96, 48))[i]
        return pltpu.make_async_remote_copy(
            src_ref=pack.at[:, 1 - core, rows], dst_ref=mate.at[:, rows],
            send_sem=r_send.at[i], recv_sem=r_recv.at[i], device_id=partner, device_id_type=MESH,
        )

    to_mate(0).start()
    g_low_twice = jnp.concatenate([g_low, g_low], axis=1).astype(BF16)
    for pair in range(half_h):
        down = dot(att[:, pl.ds(pair * 192, 192)], g_low_twice, 0, 0)
        for i in range(2):
            top, low_end = down[i * 96 : i * 96 + 48], down[i * 96 + 48 : i * 96 + 96]
            pack[pair, i, 96:144, :] = jnp.where(left, top, low_end).astype(BF16)
    to_mate(1).start()

    for i in range(2):
        to_mate(i).wait()
        rows = (pl.ds(0, 96), pl.ds(96, 48))[i]
        for j in range(half_h):
            chip[j, rows, :] = (
                pack[j, core, rows, :].astype(F32) + mate[j, rows, :].astype(F32)
            ).astype(BF16)

    takes = lax.rem(me_h, 2) == core
    slot = me_h * 2 + z_lo
    part_rows = (pl.ds(0, HALF), pl.ds(HALF, PIECE - HALF))

    def to_owner(i, zl):
        j = lax.rem(me_h // 2 + i, half_h)
        size = (HALF, PIECE - HALF)[zl]
        return pltpu.make_async_remote_copy(
            src_ref=chip.at[j, part_rows[zl]], dst_ref=got.at[slot, pl.ds(0, size)],
            send_sem=r_send.at[2 + 2 * i + zl], recv_sem=r_recv.at[2],
            device_id=(2 * zl + core, 2 * j + core, me_g), device_id_type=MESH,
        )

    for i in range(half_h):
        for zl in range(2):
            if i == 0:
                own = takes & (z_lo == zl)

                @pl.when(own)
                def _(zl=zl):
                    size = (HALF, PIECE - HALF)[zl]
                    got[slot, 0:size, :] = chip[me_h // 2, part_rows[zl], :]

                @pl.when(jnp.logical_not(own))
                def _(zl=zl):
                    to_owner(0, zl).start()
            else:
                to_owner(i, zl).start()

    for i in range(1, n_h):
        sum_h(i).wait_send()
    pltpu.make_async_copy(part_h.at[0 : n_h - 1], part_h.at[0 : n_h - 1], s_recv.at[1]).wait()
    square = part_h[0]
    for i in range(1, n_h):
        square = square + part_h[i]
    square = square[0:1, :]
    count = 4 * COLS * LAT * n_tm * n_h
    logp = -square / (2.0 * count) - HALF_LOG_TAU
    gain = adv[0]
    ratio = jnp.exp(logp - slp[0])
    low_end, high_end = 1.0 - CLIP_RANGE, 1.0 + CLIP_RANGE
    plain = -gain * ratio
    cut = -gain * jnp.clip(ratio, low_end, high_end)
    inside = jnp.where(
        (ratio > low_end) & (ratio < high_end), 1.0,
        jnp.where((ratio == low_end) | (ratio == high_end), 0.5, 0.0),
    )
    weight = jnp.where(plain > cut, 1.0, jnp.where(plain == cut, 0.5 + 0.5 * inside, inside))
    slope = weight * plain * (1.0 / n_g)

    def to_group(i):
        return pltpu.make_async_remote_copy(
            src_ref=ysum.at[me_g], dst_ref=ysum.at[me_g], send_sem=r_send.at[2 + n_h + i], recv_sem=r_recv.at[3],
            device_id=(tm, me_h, lax.rem(me_g + i, n_g)), device_id_type=MESH,
        )

    def to_tm(i):
        there = lax.rem(tm + i, n_tm)
        return pltpu.make_async_remote_copy(
            src_ref=final.at[z_lo], dst_ref=final.at[z_lo], send_sem=r_send.at[2 + n_h + n_g + i],
            recv_sem=r_recv.at[4 + z_lo], device_id=(there, me_h, me_g), device_id_type=MESH,
        )

    @pl.when(takes)
    def _():
        for zl in range(2):
            @pl.when(z_lo == zl)
            def _(zl=zl):
                arrived = got.at[0 : plane - 1, pl.ds(0, (HALF, PIECE - HALF)[zl])]
                pltpu.make_async_copy(arrived, arrived, r_recv.at[2]).wait()
        share = got[0].astype(F32)
        for i in range(1, plane):
            share = share + got[i].astype(F32)
        ysum[me_g] = (share * slope).astype(BF16)
        for i in range(1, n_g):
            to_group(i).start()
        pltpu.make_async_copy(ysum.at[0 : n_g - 1], ysum.at[0 : n_g - 1], r_recv.at[3]).wait()
        share = ysum[0].astype(F32)
        for i in range(1, n_g):
            share = share + ysum[i].astype(F32)
        final[z_lo] = share
        for i in range(1, n_tm):
            to_tm(i).start()
        other = 1 - z_lo
        pltpu.make_async_copy(final.at[other], final.at[other], r_recv.at[4 + other]).wait()
        for i in range(1, n_g):
            to_group(i).wait_send()
        for i in range(1, n_tm):
            to_tm(i).wait_send()

    @pl.when(jnp.logical_not(takes))
    def _():
        for zl in range(2):
            pltpu.make_async_copy(final.at[zl], final.at[zl], r_recv.at[4 + zl]).wait()

    out[0:HALF, :] = final[0]
    out[HALF:PIECE, :] = final[1, 0 : PIECE - HALF, :]

    for part in range(n_parts):
        when_each(sends, range(8), part, lambda copy: copy.wait_send())
    for i in range(half_h):
        for zl in range(2):
            if i == 0:
                @pl.when(jnp.logical_not(takes & (z_lo == zl)))
                def _(zl=zl):
                    to_owner(0, zl).wait_send()
            else:
                to_owner(i, zl).wait_send()


def unpack_kernel(packed, down_t, up):
    odd = lax.rem(lax.axis_index("height"), 2) == 1
    full = packed[0:64, :]
    rest = packed[64:96, :]
    narrow = jnp.concatenate([rest[:, 0:64], rest[:, 64:128]], axis=0)

    @pl.when(odd)
    def _():
        up[...] = jnp.concatenate([narrow, full], axis=1)

    @pl.when(jnp.logical_not(odd))
    def _():
        up[...] = jnp.concatenate([full, narrow], axis=1)

    down = packed[96:144, :]
    down = jnp.concatenate([down[:, 0:64], down[:, 64:128]], axis=0)
    down_t[...] = down.T


def body(
    queries, keys, values, window, adapter_down_factor, adapter_up_factor, stream, modulation,
    closing_weight, closing_bias, latent, next_latent_sample, sampling_log_probability, advantage,
):
    heads = window.shape[0]
    width = heads * HEAD
    model = stream.shape[-1]
    n_tm, n_h, n_g = lax.axis_size("tm"), lax.axis_size("height"), lax.axis_size("group")
    n_z = 4 if n_h == 16 else 2
    group_heads = 3 if heads % 3 == 0 and heads > 3 else 1
    dims = (n_tm, n_h, n_g, n_z, heads, group_heads)
    n_parts = heads // group_heads
    tokens = 4 * COLS
    vmem = pl.BlockSpec(memory_space=pltpu.VMEM)
    smem = pl.BlockSpec(memory_space=pltpu.SMEM)
    hbm = pl.BlockSpec(memory_space=pl.ANY)
    dma = pltpu.SemaphoreType.DMA
    packed = pl.pallas_call(
        functools.partial(kernel, dims),
        out_shape=jax.ShapeDtypeStruct((PIECE, 128), F32),
        in_specs=[hbm, hbm, hbm, smem, vmem, vmem, hbm, vmem, hbm, vmem, vmem, vmem, smem, smem],
        out_specs=vmem,
        scratch_shapes=[
            pltpu.VMEM((2, 2, COLS, width), BF16),
            pltpu.VMEM((2, 4, 4, COLS, width), BF16),
            pltpu.VMEM((2, 2, COLS, model), BF16),
            pltpu.VMEM((LAT, model), BF16),
            pltpu.VMEM((n_h, 2 * HALF, 128), BF16),
            pltpu.VMEM((width, 128), BF16),
            pltpu.VMEM((model, 128), BF16),
            pltpu.VMEM((tokens, width), BF16),
            pltpu.VMEM((tokens, model), F32),
            pltpu.VMEM((tokens, model), F32),
            pltpu.VMEM((n_h // 2, 2, PIECE, 128), BF16),
            pltpu.VMEM((n_h // 2, PIECE, 128), BF16),
            pltpu.VMEM((n_h // 2, PIECE, 128), BF16),
            pltpu.VMEM((2 * n_h, HALF, 128), BF16),
            pltpu.VMEM((n_g, HALF, 128), BF16),
            pltpu.VMEM((2, HALF, 128), F32),
            pltpu.VMEM((64, 128), F32),
            pltpu.VMEM((128, 128), F32),
            pltpu.VMEM((n_tm, 8, 128), F32),
            pltpu.VMEM((n_h, 8, 128), F32),
            dma((5,)),
            dma((n_parts, 8)),
            dma((n_parts, 8)),
            dma((n_h,)),
            dma((3,)),
            dma((n_tm + n_h,)),
            dma((2,)),
            dma((2 + n_h + n_g + n_tm,)),
            dma((6,)),
        ],
        compiler_params=pltpu.CompilerParams(
            collective_id=0, has_side_effects=True, vmem_limit_bytes=48 * 1024 * 1024
        ),
        name="step",
    )(
        queries, keys, values, window.T, adapter_down_factor.T, adapter_up_factor, stream,
        modulation.transpose(1, 0, 2), closing_weight.T, closing_bias.reshape(1, LAT), latent,
        next_latent_sample, sampling_log_probability, advantage,
    )
    down_t, up = pl.pallas_call(
        unpack_kernel,
        out_shape=(
            jax.ShapeDtypeStruct((RANK, DOWN_SHARD), F32),
            jax.ShapeDtypeStruct((RANK, UP_SHARD), F32),
        ),
        in_specs=[vmem],
        out_specs=(vmem, vmem),
        name="unpack",
    )(packed)
    return (down_t.T, up)


def solution(mesh):
    return jax.shard_map(
        body,
        mesh=mesh,
        in_specs=(
            P("group", "tm", "height", None, None),
            P("group", "tm", "height", None, None),
            P("group", "tm", "height", None, None),
            P(),
            P("height", None),
            P(None, "height"),
            P("group", "tm", "height", None, None),
            P("group", None, None),
            P(),
            P(),
            P("group", "tm", "height", None),
            P("group", "tm", "height", None),
            P("group"),
            P("group"),
        ),
        out_specs=(P("height", None), P(None, "height")),
        check_vma=False,
    )
```

```python
import functools
import math

import jax
import jax.numpy as jnp
from jax import lax
from jax.experimental import pallas as pl
from jax.experimental.pallas import tpu as pltpu
from jax.sharding import PartitionSpec as P

TILE_W = 8
COLS = 32
HEAD = 128
RANK = 64
LAT = 64
SAMPLER_STEP = -0.5
CLIP_RANGE = 0.2
NORM_EPS = 1e-06
HALF_LOG_TAU = 0.5 * math.log(2.0 * math.pi)
DOWN_SHARD = 96
UP_SHARD = 192
PIECE = 144
HALF = 80
FAR = 32768.0
F32 = jnp.float32
BF16 = jnp.bfloat16
MESH = pl.DeviceIdType.MESH


def dot(a, b, ca, cb):
    return lax.dot_general(a, b, (((ca,), (cb,)), ((), ())), preferred_element_type=F32)


def kernel(
    dims,
    q_hbm, k_hbm, v_hbm, win_hbm, a_hbm, b_hbm, st_hbm, mod_hbm, w_hbm, bias_hbm, lat_hbm, nxt_hbm,
    slp_hbm, adv_hbm,
    out,
    win, slp, adv, a_t, b_own, mod, bias, lat, nxt,
    q, kv, st, w_t, gath, a_full, b_full, att, even, rhs, pack, mate, chip, got, ysum, final,
    d2, dn, cross, offset, part_core, part_plane, load_sem, halo_send, halo_recv, g_send, g_recv, s_send, s_recv,
    r_send, r_recv,
):
    n_tm, n_h, n_g, n_z, heads, parts = dims
    width = heads * HEAD
    model = st.shape[-1]
    n_x = n_h // n_z
    tm, me_h, me_g = lax.axis_index("tm"), lax.axis_index("height"), lax.axis_index("group")
    core, z_lo = lax.rem(tm, 2), tm // 2
    me_x, me_z = me_h // n_z, lax.rem(me_h, n_z)
    half_h = n_h // 2
    me_h_odd = lax.rem(me_h, 2) == 1

    loads = [
        pltpu.make_async_copy(k_hbm.at[0], kv.at[0, 1:3, 1:3], load_sem.at[0]),
        pltpu.make_async_copy(v_hbm.at[0], kv.at[1, 1:3, 1:3], load_sem.at[1]),
        pltpu.make_async_copy(q_hbm.at[0], q, load_sem.at[2]),
        pltpu.make_async_copy(st_hbm.at[0], st, load_sem.at[3]),
        pltpu.make_async_copy(w_hbm, w_t, load_sem.at[4]),
    ]
    small = ((a_hbm, a_t), (b_hbm, b_own), (win_hbm, win), (mod_hbm, mod), (bias_hbm, bias), (lat_hbm, lat),
             (nxt_hbm, nxt), (slp_hbm, slp), (adv_hbm, adv))
    loads += [pltpu.make_async_copy(*ends, load_sem.at[5 + i]) for i, ends in enumerate(small)]
    first_loads, later_loads = (0, 1, 5, 6), (2, 3, 4, 7, 8, 9, 10, 11, 12, 13)
    for i in first_loads:
        loads[i].start()

    barrier = pltpu.get_barrier_semaphore()
    plane = 2 * n_h

    def greet_plane(i, _):
        at = lax.rem(me_h * 2 + z_lo + i, plane)
        pl.semaphore_signal(
            barrier, inc=1, device_id=(2 * lax.rem(at, 2) + core, at // 2, me_g), device_id_type=MESH
        )
        return 0

    lax.fori_loop(1, plane, greet_plane, 0)

    def greet_group(i, _):
        pl.semaphore_signal(
            barrier, inc=1, device_id=(tm, me_h, lax.rem(me_g + i, n_g)), device_id_type=MESH
        )
        return 0

    lax.fori_loop(1, n_g, greet_group, 0)
    for zl in range(2):
        pl.semaphore_signal(
            barrier, inc=1, device_id=(2 * zl + 1 - core, me_h, me_g), device_id_type=MESH
        )
        for step_h in (1, n_h - 1):
            pl.semaphore_signal(
                barrier, inc=1, device_id=(2 * zl + 1 - core, lax.rem(me_h + step_h, n_h), me_g),
                device_id_type=MESH,
            )

    lane = lax.broadcasted_iota(jnp.int32, (1, 128), 1)
    left = lane < 64
    unit_row = lax.broadcasted_iota(jnp.int32, (64, 128), 0)
    unit_lane = lax.broadcasted_iota(jnp.int32, (64, 128), 1)
    loads[5].wait()
    loads[6].wait()
    twice = (lax.rem(unit_lane, 64) == unit_row).astype(F32).astype(BF16)
    a_rows = dot(a_t[...], twice, 0, 0)
    b_wide = b_own[...].astype(F32)
    b_even, b_odd = b_wide[:, 0:128], b_wide[:, 64:192]
    edge = jnp.where(me_h_odd, b_wide[:, 0:64], b_wide[:, 128:192])
    own_rows = jnp.concatenate(
        [
            jnp.where(me_h_odd, b_odd, b_even),
            jnp.concatenate([edge[0:32], edge[32:64]], axis=1),
            jnp.where(left, a_rows[0:48], a_rows[48:96]),
        ],
        axis=0,
    ).astype(BF16)

    @pl.when(core == 0)
    def _():
        gath[me_h, 0:HALF, :] = own_rows[0:HALF]

    @pl.when(core == 1)
    def _():
        gath[me_h, HALF:PIECE, :] = own_rows[HALF:PIECE]

    first_tm, last_tm = tm == 0, tm == n_tm - 1
    first_h, last_h = me_h == 0, me_h == n_h - 1

    @pl.when(first_tm)
    def _():
        kv[:, 0:1] = jnp.zeros((2, 1, 4, COLS, width), BF16)

    @pl.when(last_tm)
    def _():
        kv[:, 3:4] = jnp.zeros((2, 1, 4, COLS, width), BF16)

    @pl.when(first_h)
    def _():
        kv[:, :, 0:1] = jnp.zeros((2, 4, 1, COLS, width), BF16)

    @pl.when(last_h)
    def _():
        kv[:, :, 3:4] = jnp.zeros((2, 4, 1, COLS, width), BF16)

    loads[0].wait()
    loads[1].wait()
    pl.semaphore_wait(barrier, plane - 1 + n_g - 1 + 6)

    n_parts = len(parts)
    firsts = [sum(parts[:i]) for i in range(n_parts + 1)]
    ahead_h = (tm, jnp.minimum(me_h + 1, n_h - 1), me_g)
    back_h = (tm, jnp.maximum(me_h - 1, 0), me_g)
    ahead_tm = (jnp.minimum(tm + 1, n_tm - 1), me_h, me_g)
    back_tm = (jnp.maximum(tm - 1, 0), me_h, me_g)

    def lanes(i, size):
        return pl.ds(pl.multiple_of(i * size, 128), size)

    def halo(part, way):
        cols = pl.ds(firsts[part] * HEAD, parts[part] * HEAD)
        src, dst, to = {
            0: (kv.at[:, 1:3, 2, :, cols], kv.at[:, 1:3, 0, :, cols], ahead_h),
            1: (kv.at[:, 1:3, 1, :, cols], kv.at[:, 1:3, 3, :, cols], back_h),
            2: (kv.at[:, 2, 1:3, :, cols], kv.at[:, 0, 1:3, :, cols], ahead_tm),
            3: (kv.at[:, 1, 1:3, :, cols], kv.at[:, 3, 1:3, :, cols], back_tm),
            4: (kv.at[:, 2, 0, :, cols], kv.at[:, 0, 0, :, cols], ahead_tm),
            5: (kv.at[:, 1, 0, :, cols], kv.at[:, 3, 0, :, cols], back_tm),
            6: (kv.at[:, 2, 3, :, cols], kv.at[:, 0, 3, :, cols], ahead_tm),
            7: (kv.at[:, 1, 3, :, cols], kv.at[:, 3, 3, :, cols], back_tm),
            8: (kv.at[:, 2, 2, :, cols], kv.at[:, 0, 0, :, cols], (ahead_tm[0], ahead_h[1], me_g)),
            9: (kv.at[:, 1, 2, :, cols], kv.at[:, 3, 0, :, cols], (back_tm[0], ahead_h[1], me_g)),
            10: (kv.at[:, 2, 1, :, cols], kv.at[:, 0, 3, :, cols], (ahead_tm[0], back_h[1], me_g)),
            11: (kv.at[:, 1, 1, :, cols], kv.at[:, 3, 3, :, cols], (back_tm[0], back_h[1], me_g)),
        }[way]
        return pltpu.make_async_remote_copy(
            src_ref=src, dst_ref=dst, send_sem=halo_send.at[part, way], recv_sem=halo_recv.at[part, way],
            device_id=to, device_id_type=MESH,
        )

    not_first_tm, not_last_tm = tm > 0, tm < n_tm - 1
    not_first_h, not_last_h = me_h > 0, me_h < n_h - 1
    sends = {
        0: not_last_h, 1: not_first_h, 2: not_last_tm, 3: not_first_tm,
        4: not_first_h & not_last_tm, 5: not_first_h & not_first_tm,
        6: not_last_h & not_last_tm, 7: not_last_h & not_first_tm,
        8: not_last_h & not_last_tm, 9: not_last_h & not_first_tm,
        10: not_first_h & not_last_tm, 11: not_first_h & not_first_tm,
    }
    receives = {
        0: not_first_h, 1: not_last_h, 2: not_first_tm, 3: not_last_tm,
        4: not_first_h & not_first_tm, 5: not_first_h & not_last_tm,
        6: not_last_h & not_first_tm, 7: not_last_h & not_last_tm,
        8: not_first_h & not_first_tm, 9: not_first_h & not_last_tm,
        10: not_last_h & not_first_tm, 11: not_last_h & not_last_tm,
    }

    def when_each(table, ways, part, act):
        for way in ways:
            @pl.when(table[way])
            def _(way=way):
                act(halo(part, way))

    def first_ways(part):
        return (0, 1, 2, 3) + ((8, 9, 10, 11) if part == n_parts - 1 else ())

    def second_ways(part):
        return () if part == n_parts - 1 else (4, 5, 6, 7)

    def late_ways(part):
        return (2, 3) + (second_ways(part) or (8, 9, 10, 11))

    def leave():
        for part in range(n_parts):
            when_each(sends, first_ways(part) + second_ways(part), part, lambda copy: copy.wait_send())

    my_rows = pl.ds(pl.multiple_of(core * HALF, 16), HALF)

    def gather_z(i):
        src = gath.at[me_h, my_rows]
        to = (tm, me_x * n_z + lax.rem(me_z + i, n_z), me_g)
        return pltpu.make_async_remote_copy(
            src_ref=src, dst_ref=src, send_sem=g_send.at[i], recv_sem=g_recv.at[0],
            device_id=to, device_id_type=MESH,
        )

    def gather_x(i):
        src = gath.at[pl.ds(me_x * n_z, n_z), my_rows]
        to = (tm, lax.rem(me_x + i, n_x) * n_z + me_z, me_g)
        return pltpu.make_async_remote_copy(
            src_ref=src, dst_ref=src, send_sem=g_send.at[n_z + i], recv_sem=g_recv.at[1],
            device_id=to, device_id_type=MESH,
        )

    def gather_core():
        src = gath.at[:, my_rows]
        return pltpu.make_async_remote_copy(
            src_ref=src, dst_ref=src, send_sem=g_send.at[0], recv_sem=g_recv.at[2],
            device_id=(2 * z_lo + 1 - core, me_h, me_g), device_id_type=MESH,
        )

    for i in range(1, n_z):
        gather_z(i).start()

    for part in range(n_parts):
        when_each(sends, first_ways(part), part, lambda copy: copy.start())
    for i in later_loads:
        loads[i].start()

    tokens = 4 * COLS
    q_at = lax.broadcasted_iota(jnp.int32, (tokens, 128), 0)
    feature = lax.broadcasted_iota(jnp.int32, (tokens, 128), 1)
    q_frame, q_row, q_tile = q_at // 64, lax.rem(q_at // 32, 2), lax.rem(q_at, 32) // TILE_W
    frame_at = tm * 2 - 1 + feature
    row_at = me_h * 2 - 1 + (feature - 4)
    gap_frame = jnp.where(
        (frame_at >= 0) & (frame_at < 2 * n_tm), jnp.abs(q_frame + 1 - feature), 99
    )
    gap_row = jnp.where(
        (row_at >= 0) & (row_at < 2 * n_h), jnp.abs(q_row + 1 - (feature - 4)), 99
    )
    gap_tile = jnp.abs(q_tile - (feature - 8))
    gap = jnp.where(
        feature < 4, gap_frame,
        jnp.where(feature < 8, gap_row, jnp.where(feature < 12, gap_tile, -1)),
    )
    k_at = lax.broadcasted_iota(jnp.int32, (512, 128), 0)
    k_feature = lax.broadcasted_iota(jnp.int32, (512, 128), 1)
    k_one_hot = (
        (k_feature == k_at // 128)
        | (k_feature == 4 + lax.rem(k_at // 32, 4))
        | (k_feature == 8 + lax.rem(k_at, 32) // TILE_W)
    ).astype(F32).astype(BF16)
    ones = jnp.ones((512, 128), BF16)
    factor = HEAD**-0.5 * math.log2(math.e)

    def attend(part):
        for head in range(firsts[part], firsts[part + 1]):
            cols = pl.ds(head * HEAD, HEAD)
            reach = jnp.where(
                lane < 4, win[0, head], jnp.where(lane < 8, win[1, head], win[2, head])
            )
            penalty = jnp.where(gap > reach, -FAR, 0.0).astype(BF16)
            query = jnp.concatenate([q[:, :, :, cols].reshape(tokens, HEAD), penalty], axis=1)
            key = jnp.concatenate([kv[0, :, :, :, cols].reshape(512, HEAD), k_one_hot], axis=1)
            scores = dot(query, key, 1, 1)
            top = jnp.max(scores, axis=1, keepdims=True)
            terms = jnp.exp2((scores - top) * factor).astype(BF16)
            value = jnp.concatenate([kv[1, :, :, :, cols].reshape(512, HEAD), ones], axis=1)
            mixed = dot(terms, value, 1, 0)
            att[:, cols] = (mixed[:, :HEAD] / mixed[:, HEAD:]).astype(BF16)

    step = 2 * UP_SHARD
    n_pairs = model // step

    def unrolled(carry, act):
        for i in range(n_pairs):
            carry = act(i, pl.ds(i * step, step), carry)
        return carry

    def sweep(carry, act):
        return lax.fori_loop(0, n_pairs, lambda i, c: act(i, lanes(i, step), c), carry)

    def fold(x):
        total = x[:, 0:128]
        for i in range(1, x.shape[1] // 128):
            total = total + x[:, i * 128 : (i + 1) * 128]
        return total

    def mean(total):
        return jnp.sum(total, axis=1, keepdims=True) * (1.0 / model)

    def prepare():
        def sums(_, cols, carry):
            sum_s, sum_w, sum_b, sum_c = carry
            wide = w_t[:, cols].astype(F32)
            return (
                sum_s + fold(st[:, :, :, cols].reshape(tokens, step).astype(F32)),
                sum_w + fold(wide * (1.0 + mod[2, :, cols])),
                sum_b + fold(b_full[:, cols].astype(F32) * mod[0, :, cols]),
                sum_c + fold(wide * mod[1, :, cols]),
            )

        narrow = jnp.zeros((LAT, 128), F32)
        sum_s, sum_w, sum_b, sum_c = sweep((jnp.zeros((tokens, 128), F32), narrow, narrow, narrow), sums)
        mean_s, mean_w, mean_b = mean(sum_s), mean(sum_w), mean(sum_b)

        def centre(_, cols, product):
            even[:, cols] = st[:, :, :, cols].reshape(tokens, step).astype(F32) - mean_s
            scaled_w = (w_t[:, cols].astype(F32) * (1.0 + mod[2, :, cols]) - mean_w).astype(BF16)
            scaled_b = (b_full[:, cols].astype(F32) * mod[0, :, cols] - mean_b).astype(BF16)
            rhs[0:64, cols] = scaled_w
            rhs[64:128, cols] = scaled_b
            return product + dot(scaled_w, scaled_b, 1, 1)

        cross[:, 0:RANK] = sweep(jnp.zeros((LAT, RANK), F32), centre).astype(BF16)
        constant = jnp.sum(sum_c, axis=1, keepdims=True)
        shift = jnp.sum(jnp.where(unit_row == unit_lane, constant, 0.0), axis=0, keepdims=True)
        offset[...] = shift + jnp.concatenate([bias[...], jnp.zeros((1, 64), F32)], axis=1)

    last_cols = firsts[-2] * HEAD

    def spread_x():
        for i in range(1, n_z):
            gather_z(i).wait_send()
        taken = gath.at[pl.ds(0, n_z - 1), my_rows]
        pltpu.make_async_copy(taken, taken, g_recv.at[0]).wait()
        for i in range(1, n_x):
            gather_x(i).start()

    def spread_core():
        for i in range(1, n_x):
            gather_x(i).wait_send()
        taken = gath.at[pl.ds(0, (n_x - 1) * n_z), my_rows]
        pltpu.make_async_copy(taken, taken, g_recv.at[1]).wait()
        gather_core().start()

    def lay_out():
        gather_core().wait()
        for i in later_loads:
            if i not in (2, 7):
                loads[i].wait()

        def adapter(pair, _):
            for i in range(2):
                both = gath[2 * pair + i, 96:144, :]
                at = pl.multiple_of((2 * pair + i) * 96, 16)
                a_full[pl.ds(at, 48), :] = both
                a_full[pl.ds(at + 48, 48), 0:64] = both[:, 64:128]
            at = pl.multiple_of(pair * step, 128)
            b_full[:, pl.ds(at, 128)] = gath[2 * pair, 0:64, :]
            b_full[:, pl.ds(at + 256, 128)] = gath[2 * pair + 1, 0:64, :]
            first = gath[2 * pair, 64:96, :].astype(F32)
            second = gath[2 * pair + 1, 64:96, :].astype(F32)
            b_full[0:32, pl.ds(at + 128, 128)] = jnp.where(
                left, first, pltpu.roll(second, 64, 1)
            ).astype(BF16)
            b_full[32:64, pl.ds(at + 128, 128)] = jnp.where(
                left, pltpu.roll(first, 64, 1), second
            ).astype(BF16)
            return 0

        lax.fori_loop(0, half_h, adapter, 0)
        for f in range(2):
            for j in range(16):
                cols = pl.ds(j * 128, 128)
                d2[pl.ds(f * 32 + 2 * j, 2), :] = nxt[0, f, :, cols] - lat[0, f, :, cols]
        for f in range(2):
            for r in range(2):
                pair = d2[pl.ds(f * 32 + r, 16, stride=2), :]
                dn[pl.ds(f * 64 + r * 32, 16, stride=2), :] = pair
                dn[pl.ds(f * 64 + r * 32 + 1, 16, stride=2), :] = pltpu.roll(pair, 64, 1)
        prepare()

    def arrive(part):
        when_each(receives, (0, 1), part, lambda copy: copy.wait_recv())
        when_each(sends, second_ways(part), part, lambda copy: copy.start())

    def finish_part(part):
        when_each(receives, late_ways(part), part, lambda copy: copy.wait_recv())
        attend(part)

    for i in (2, 7):
        loads[i].wait()
    arrive(0)
    spread_x()
    arrive(1)
    spread_core()
    for part in range(2, n_parts - 1):
        arrive(part)
    lay_out()
    for part in range(n_parts - 1):
        finish_part(part)
    low_sum = dot(att[:, 0:last_cols], a_full[0:last_cols, 0:64], 1, 0)
    arrive(n_parts - 1)
    finish_part(n_parts - 1)
    low = (low_sum + dot(att[:, last_cols:width], a_full[last_cols:width, 0:64], 1, 0)).astype(BF16)

    def forward(_, cols, carry):
        total, seen = carry
        apart = even[:, cols] + dot(low, rhs[64:128, cols], 1, 0)
        narrow = apart.astype(BF16)
        rhs[128:256, cols] = narrow
        return total + fold(apart * apart), seen + dot(narrow, rhs[0:128, cols], 1, 1)

    blank = jnp.zeros((tokens, 128), F32)
    total, seen = unrolled((blank, blank), forward)
    inverse = lax.rsqrt(mean(total) + NORM_EPS)
    by_weight = jnp.where(left, inverse * seen, 0.0)
    by_up = pltpu.roll(seen, 64, 1)[:, 0:64]
    residue = jnp.where(left, dn[...] - SAMPLER_STEP * (by_weight + offset[...]), 0.0)

    square = jnp.sum(jnp.sum(residue * residue, axis=0, keepdims=True), axis=1, keepdims=True)
    part_core[core] = jnp.broadcast_to(square, (8, 128))
    partner = (2 * z_lo + 1 - core, me_h, me_g)

    def sum_core():
        return pltpu.make_async_remote_copy(
            src_ref=part_core.at[core], dst_ref=part_core.at[core], send_sem=s_send.at[0], recv_sem=s_recv.at[0],
            device_id=partner, device_id_type=MESH,
        )

    sum_core().start()

    g_velocity = SAMPLER_STEP * residue
    along = inverse * (jnp.sum(g_velocity * by_weight, axis=1, keepdims=True) * (1.0 / model))
    by_token = (-(inverse * along) * low.astype(F32)).T.astype(BF16)
    by_lat = dot(low, (inverse * g_velocity).astype(BF16), 0, 0).astype(BF16)
    lhs = jnp.concatenate([by_lat, by_token], axis=1)

    def share_up(pair, cols, carry):
        up = mod[0, :, cols] * dot(lhs, rhs[:, cols], 1, 0)
        pack[pair, 0, 0:64, :] = up[:, 0:128].astype(BF16)
        pack[pair, 1, 0:64, :] = up[:, 256:384].astype(BF16)
        shared = up[:, 128:256]
        turned = pltpu.roll(shared, 64, 1)
        pack[pair, 0, 64:96, :] = jnp.where(left, shared[0:32], turned[32:64]).astype(BF16)
        pack[pair, 1, 64:96, :] = jnp.where(left, turned[0:32], shared[32:64]).astype(BF16)
        return carry

    unrolled(0, share_up)

    def to_mate(i):
        rows = (pl.ds(0, 96), pl.ds(96, 48))[i]
        return pltpu.make_async_remote_copy(
            src_ref=pack.at[:, 1 - core, rows], dst_ref=mate.at[:, rows],
            send_sem=r_send.at[i], recv_sem=r_recv.at[i], device_id=partner, device_id_type=MESH,
        )

    to_mate(0).start()
    g_low = inverse * (dot(g_velocity[:, 0:64].astype(BF16), cross[:, 0:RANK], 1, 0) - along * by_up)
    g_low_twice = jnp.concatenate([g_low, g_low], axis=1).astype(BF16)

    def share_down(pair, _):
        down = dot(att[:, pl.ds(pl.multiple_of(pair * 384, 128), 384)], g_low_twice, 0, 0)
        for i in range(4):
            top, low_end = down[i * 96 : i * 96 + 48], down[i * 96 + 48 : i * 96 + 96]
            pack[2 * pair + i // 2, i % 2, 96:144, :] = jnp.where(left, top, low_end).astype(BF16)
        return 0

    lax.fori_loop(0, half_h // 2, share_down, 0)
    to_mate(1).start()

    def add_mate(i):
        to_mate(i).wait()
        rows = (pl.ds(0, 96), pl.ds(96, 48))[i]

        def add(j, _):
            chip[j, rows, :] = (
                pack[j, core, rows, :].astype(F32) + mate[j, rows, :].astype(F32)
            ).astype(BF16)
            return 0

        lax.fori_loop(0, half_h, add, 0)

    takes = lax.rem(me_h, 2) == core
    slot = me_h * 2 + z_lo
    part_rows = (pl.ds(0, HALF), pl.ds(HALF, PIECE - HALF))

    def to_owner(i, zl):
        j = lax.rem(me_h // 2 + i, half_h)
        size = (HALF, PIECE - HALF)[zl]
        return pltpu.make_async_remote_copy(
            src_ref=chip.at[j, part_rows[zl]], dst_ref=got.at[slot, pl.ds(0, size)],
            send_sem=r_send.at[2 + 2 * i + zl], recv_sem=r_recv.at[2],
            device_id=(2 * zl + core, 2 * j + core, me_g), device_id_type=MESH,
        )

    def sum_owner(i, zl):
        j = lax.rem(me_h // 2 + i, half_h)
        return pltpu.make_async_remote_copy(
            src_ref=part_plane.at[slot], dst_ref=part_plane.at[slot], send_sem=s_send.at[1 + 2 * i + zl],
            recv_sem=s_recv.at[1], device_id=(2 * zl + core, 2 * j + core, me_g), device_id_type=MESH,
        )

    def for_owners(zl, act):
        @pl.when(jnp.logical_not(takes & (z_lo == zl)))
        def _():
            act(0, zl)

        for i in range(1, half_h):
            act(i, zl)

    sum_core().wait()
    part_plane[slot] = part_core[0] + part_core[1]
    for zl in range(2):
        for_owners(zl, lambda i, zl: sum_owner(i, zl).start())

    for zl in range(2):
        add_mate(zl)
        own = takes & (z_lo == zl)

        @pl.when(own)
        def _(zl=zl):
            size = (HALF, PIECE - HALF)[zl]
            got[slot, 0:size, :] = chip[me_h // 2, part_rows[zl], :]

        for_owners(zl, lambda i, zl: to_owner(i, zl).start())

    def to_group(i):
        return pltpu.make_async_remote_copy(
            src_ref=ysum.at[me_g], dst_ref=ysum.at[me_g], send_sem=r_send.at[2 + n_h + i], recv_sem=r_recv.at[3],
            device_id=(tm, me_h, lax.rem(me_g + i, n_g)), device_id_type=MESH,
        )

    def to_tm(i):
        there = lax.rem(tm + i, n_tm)
        return pltpu.make_async_remote_copy(
            src_ref=final.at[z_lo], dst_ref=final.at[z_lo], send_sem=r_send.at[2 + n_h + n_g + i],
            recv_sem=r_recv.at[4 + z_lo], device_id=(there, me_h, me_g), device_id_type=MESH,
        )

    @pl.when(takes)
    def _():
        arrived = part_plane.at[0 : plane - 1]
        pltpu.make_async_copy(arrived, arrived, s_recv.at[1]).wait()
        square = part_plane[0]
        for i in range(1, plane):
            square = square + part_plane[i]
        square = square[0:1, :]
        count = 4 * COLS * LAT * n_tm * n_h
        logp = -square / (2.0 * count) - HALF_LOG_TAU
        gain = adv[0]
        ratio = jnp.exp(logp - slp[0])
        low_end, high_end = 1.0 - CLIP_RANGE, 1.0 + CLIP_RANGE
        plain = -gain * ratio
        cut = -gain * jnp.clip(ratio, low_end, high_end)
        inside = jnp.where(
            (ratio > low_end) & (ratio < high_end), 1.0,
            jnp.where((ratio == low_end) | (ratio == high_end), 0.5, 0.0),
        )
        weight = jnp.where(plain > cut, 1.0, jnp.where(plain == cut, 0.5 + 0.5 * inside, inside))
        slope = weight * plain * (1.0 / n_g)

        for zl in range(2):
            @pl.when(z_lo == zl)
            def _(zl=zl):
                arrived = got.at[0 : plane - 1, pl.ds(0, (HALF, PIECE - HALF)[zl])]
                pltpu.make_async_copy(arrived, arrived, r_recv.at[2]).wait()
        share = lax.fori_loop(
            0, plane // 4,
            lambda i, sofar: sofar
            + ((got[4 * i].astype(F32) + got[4 * i + 1].astype(F32))
               + (got[4 * i + 2].astype(F32) + got[4 * i + 3].astype(F32))),
            jnp.zeros((HALF, 128), F32),
        )
        ysum[me_g] = (share * slope).astype(BF16)
        for i in range(1, n_g):
            to_group(i).start()
        pltpu.make_async_copy(ysum.at[0 : n_g - 1], ysum.at[0 : n_g - 1], r_recv.at[3]).wait()
        share = ysum[0].astype(F32)
        for i in range(1, n_g):
            share = share + ysum[i].astype(F32)
        final[z_lo] = share
        for i in range(1, n_tm):
            to_tm(i).start()
        other = 1 - z_lo
        pltpu.make_async_copy(final.at[other], final.at[other], r_recv.at[4 + other]).wait()
        for i in range(1, n_g):
            to_group(i).wait_send()
        for i in range(1, n_tm):
            to_tm(i).wait_send()

    @pl.when(jnp.logical_not(takes))
    def _():
        for zl in range(2):
            pltpu.make_async_copy(final.at[zl], final.at[zl], r_recv.at[4 + zl]).wait()

    out[0:HALF, :] = final[0]
    out[HALF:PIECE, :] = final[1, 0 : PIECE - HALF, :]

    leave()
    for zl in range(2):
        for_owners(zl, lambda i, zl: (to_owner(i, zl).wait_send(), sum_owner(i, zl).wait_send()))


def unpack_kernel(packed, down_t, up):
    odd = lax.rem(lax.axis_index("height"), 2) == 1
    full = packed[0:64, :]
    rest = packed[64:96, :]
    narrow = jnp.concatenate([rest[:, 0:64], rest[:, 64:128]], axis=0)

    @pl.when(odd)
    def _():
        up[...] = jnp.concatenate([narrow, full], axis=1)

    @pl.when(jnp.logical_not(odd))
    def _():
        up[...] = jnp.concatenate([full, narrow], axis=1)

    down = packed[96:144, :]
    down = jnp.concatenate([down[:, 0:64], down[:, 64:128]], axis=0)
    down_t[...] = down.T


def body(
    queries, keys, values, window, adapter_down_factor, adapter_up_factor, stream, modulation,
    closing_weight, closing_bias, latent, next_latent_sample, sampling_log_probability, advantage,
):
    heads = window.shape[0]
    width = heads * HEAD
    model = stream.shape[-1]
    n_tm, n_h, n_g = lax.axis_size("tm"), lax.axis_size("height"), lax.axis_size("group")
    n_z = 4 if n_h == 16 else 2
    parts = (4, 4, 3, 1) if heads == 12 else (1,) * heads
    dims = (n_tm, n_h, n_g, n_z, heads, parts)
    n_parts = len(parts)
    tokens = 4 * COLS
    vmem = pl.BlockSpec(memory_space=pltpu.VMEM)
    hbm = pl.BlockSpec(memory_space=pl.ANY)
    dma = pltpu.SemaphoreType.DMA
    packed = pl.pallas_call(
        functools.partial(kernel, dims),
        out_shape=jax.ShapeDtypeStruct((PIECE, 128), F32),
        in_specs=[hbm] * 14,
        out_specs=vmem,
        scratch_shapes=[
            pltpu.SMEM((3, heads), jnp.int32),
            pltpu.SMEM((1,), F32),
            pltpu.SMEM((1,), F32),
            pltpu.VMEM((RANK, DOWN_SHARD), BF16),
            pltpu.VMEM((RANK, UP_SHARD), BF16),
            pltpu.VMEM((3, 1, model), F32),
            pltpu.VMEM((1, LAT), F32),
            pltpu.VMEM((1, 2, 2, COLS * LAT), F32),
            pltpu.VMEM((1, 2, 2, COLS * LAT), F32),
            pltpu.VMEM((2, 2, COLS, width), BF16),
            pltpu.VMEM((2, 4, 4, COLS, width), BF16),
            pltpu.VMEM((2, 2, COLS, model), BF16),
            pltpu.VMEM((LAT, model), BF16),
            pltpu.VMEM((n_h, 2 * HALF, 128), BF16),
            pltpu.VMEM((width, 128), BF16),
            pltpu.VMEM((RANK, model), BF16),
            pltpu.VMEM((tokens, width), BF16),
            pltpu.VMEM((tokens, model), F32),
            pltpu.VMEM((256, model), BF16),
            pltpu.VMEM((n_h // 2, 2, PIECE, 128), BF16),
            pltpu.VMEM((n_h // 2, PIECE, 128), BF16),
            pltpu.VMEM((n_h // 2, PIECE, 128), BF16),
            pltpu.VMEM((2 * n_h, HALF, 128), BF16),
            pltpu.VMEM((n_g, HALF, 128), BF16),
            pltpu.VMEM((2, HALF, 128), F32),
            pltpu.VMEM((64, 128), F32),
            pltpu.VMEM((128, 128), F32),
            pltpu.VMEM((LAT, 128), BF16),
            pltpu.VMEM((1, 128), F32),
            pltpu.VMEM((2, 8, 128), F32),
            pltpu.VMEM((2 * n_h, 8, 128), F32),
            dma((14,)),
            dma((n_parts, 12)),
            dma((n_parts, 12)),
            dma((n_h,)),
            dma((3,)),
            dma((1 + n_h,)),
            dma((2,)),
            dma((2 + n_h + n_g + n_tm,)),
            dma((6,)),
        ],
        compiler_params=pltpu.CompilerParams(
            collective_id=0, has_side_effects=True, vmem_limit_bytes=63 * 1024 * 1024
        ),
        name="step",
    )(
        queries, keys, values, window.T, adapter_down_factor.T, adapter_up_factor, stream,
        modulation.transpose(1, 0, 2), closing_weight.T, closing_bias.reshape(1, LAT), latent,
        next_latent_sample, sampling_log_probability, advantage,
    )
    down_t, up = pl.pallas_call(
        unpack_kernel,
        out_shape=(
            jax.ShapeDtypeStruct((RANK, DOWN_SHARD), F32),
            jax.ShapeDtypeStruct((RANK, UP_SHARD), F32),
        ),
        in_specs=[vmem],
        out_specs=(vmem, vmem),
        name="unpack",
    )(packed)
    return (down_t.T, up)


def solution(mesh):
    return jax.shard_map(
        body,
        mesh=mesh,
        in_specs=(
            P("group", "tm", "height", None, None),
            P("group", "tm", "height", None, None),
            P("group", "tm", "height", None, None),
            P(),
            P("height", None),
            P(None, "height"),
            P("group", "tm", "height", None, None),
            P("group", None, None),
            P(),
            P(),
            P("group", "tm", "height", None),
            P("group", "tm", "height", None),
            P("group"),
            P("group"),
        ),
        out_specs=(P("height", None), P(None, "height")),
        check_vma=False,
    )
```

```python
import functools
import math

import jax
import jax.numpy as jnp
from jax import lax
from jax.experimental import pallas as pl
from jax.experimental.pallas import tpu as pltpu
from jax.sharding import PartitionSpec as P

TILE_W = 8
COLS = 32
HEAD = 128
RANK = 64
LAT = 64
SAMPLER_STEP = -0.5
CLIP_RANGE = 0.2
NORM_EPS = 1e-06
HALF_LOG_TAU = 0.5 * math.log(2.0 * math.pi)
DOWN_SHARD = 96
UP_SHARD = 192
PIECE = 144
HALF = 80
FAR = 32768.0
F32 = jnp.float32
BF16 = jnp.bfloat16
MESH = pl.DeviceIdType.MESH


def dot(a, b, ca, cb):
    return lax.dot_general(a, b, (((ca,), (cb,)), ((), ())), preferred_element_type=F32)


def kernel(
    dims,
    q_hbm, k_hbm, v_hbm, win_hbm, a_hbm, b_hbm, st_hbm, mod_hbm, w_hbm, bias_hbm, lat_hbm, nxt_hbm,
    slp_hbm, adv_hbm,
    out,
    win, slp, adv, a_t, b_own, mod, bias, lat, nxt,
    q, kv, st, w_t, gath, a_full, b_full, att, even, rhs, pack, mate, chip, got, ysum, final,
    d2, dn, cross, offset, part_core, part_plane, load_sem, halo_send, halo_recv, g_send, g_recv, s_send, s_recv,
    r_send, r_recv, across,
):
    n_tm, n_h, n_g, n_z, heads, parts = dims
    width = heads * HEAD
    model = st.shape[-1]
    n_x = n_h // n_z
    tm, me_h, me_g = lax.axis_index("tm"), lax.axis_index("height"), lax.axis_index("group")
    core, z_lo = lax.rem(tm, 2), tm // 2
    me_x, me_z = me_h // n_z, lax.rem(me_h, n_z)
    half_h = n_h // 2
    me_h_odd = lax.rem(me_h, 2) == 1

    loads = [
        pltpu.make_async_copy(k_hbm.at[0], kv.at[0, 1:3, 1:3], load_sem.at[0]),
        pltpu.make_async_copy(v_hbm.at[0], kv.at[1, 1:3, 1:3], load_sem.at[1]),
        pltpu.make_async_copy(q_hbm.at[0], q, load_sem.at[2]),
        pltpu.make_async_copy(st_hbm.at[0], st, load_sem.at[3]),
        pltpu.make_async_copy(w_hbm, w_t, load_sem.at[4]),
    ]
    small = ((a_hbm, a_t), (b_hbm, b_own), (win_hbm, win), (mod_hbm, mod), (bias_hbm, bias), (lat_hbm, lat),
             (nxt_hbm, nxt), (slp_hbm, slp), (adv_hbm, adv))
    loads += [pltpu.make_async_copy(*ends, load_sem.at[5 + i]) for i, ends in enumerate(small)]
    first_loads, later_loads = (0, 1, 5, 6), (2, 3, 4, 7, 8, 9, 10, 11, 12, 13)
    for i in first_loads:
        loads[i].start()

    barrier = pltpu.get_barrier_semaphore()
    plane = 2 * n_h

    def greet(height, at_tm):
        pl.semaphore_signal(barrier, inc=1, device_id=(at_tm, height, me_g), device_id_type=MESH)

    for i in range(1, n_z):
        greet(me_x * n_z + lax.rem(me_z + i, n_z), tm)
    for i in range(1, n_x):
        greet(lax.rem(me_x + i, n_x) * n_z + me_z, tm)
    greet(me_h, lax.rem(tm + 2, n_tm))
    crosses = (me_z == n_z - 1, me_z == 0)

    @pl.when(crosses[0])
    def _():
        greet(lax.rem(me_h + 1, n_h), tm)

    @pl.when(crosses[1])
    def _():
        greet(lax.rem(me_h + n_h - 1, n_h), tm)


    def greet_group(i, _):
        pl.semaphore_signal(
            barrier, inc=1, device_id=(tm, me_h, lax.rem(me_g + i, n_g)), device_id_type=MESH
        )
        return 0

    lax.fori_loop(1, n_g, greet_group, 0)
    for zl in range(2):
        pl.semaphore_signal(
            barrier, inc=1, device_id=(2 * zl + 1 - core, me_h, me_g), device_id_type=MESH
        )
        for step_h in (1, n_h - 1):
            pl.semaphore_signal(
                barrier, inc=1, device_id=(2 * zl + 1 - core, lax.rem(me_h + step_h, n_h), me_g),
                device_id_type=MESH,
            )

    lane = lax.broadcasted_iota(jnp.int32, (1, 128), 1)
    left = lane < 64
    unit_row = lax.broadcasted_iota(jnp.int32, (64, 128), 0)
    unit_lane = lax.broadcasted_iota(jnp.int32, (64, 128), 1)
    loads[5].wait()
    loads[6].wait()
    twice = (lax.rem(unit_lane, 64) == unit_row).astype(F32).astype(BF16)
    a_rows = dot(a_t[...], twice, 0, 0)
    b_wide = b_own[...].astype(F32)
    b_even, b_odd = b_wide[:, 0:128], b_wide[:, 64:192]
    edge = jnp.where(me_h_odd, b_wide[:, 0:64], b_wide[:, 128:192])
    own_rows = jnp.concatenate(
        [
            jnp.where(me_h_odd, b_odd, b_even),
            jnp.concatenate([edge[0:32], edge[32:64]], axis=1),
            jnp.where(left, a_rows[0:48], a_rows[48:96]),
        ],
        axis=0,
    ).astype(BF16)

    @pl.when(core == 0)
    def _():
        gath[me_h, 0:HALF, :] = own_rows[0:HALF]

    @pl.when(core == 1)
    def _():
        gath[me_h, HALF:PIECE, :] = own_rows[HALF:PIECE]

    first_tm, last_tm = tm == 0, tm == n_tm - 1
    first_h, last_h = me_h == 0, me_h == n_h - 1

    @pl.when(first_tm)
    def _():
        kv[:, 0:1] = jnp.zeros((2, 1, 4, COLS, width), BF16)

    @pl.when(last_tm)
    def _():
        kv[:, 3:4] = jnp.zeros((2, 1, 4, COLS, width), BF16)

    @pl.when(first_h)
    def _():
        kv[:, :, 0:1] = jnp.zeros((2, 4, 1, COLS, width), BF16)

    @pl.when(last_h)
    def _():
        kv[:, :, 3:4] = jnp.zeros((2, 4, 1, COLS, width), BF16)

    loads[0].wait()
    loads[1].wait()
    crossing = crosses[0].astype(jnp.int32) + crosses[1].astype(jnp.int32)
    pl.semaphore_wait(barrier, n_z - 1 + n_x - 1 + 1 + n_g - 1 + 6 + crossing)

    n_parts = len(parts)
    firsts = [sum(parts[:i]) for i in range(n_parts + 1)]
    ahead_h = (tm, jnp.minimum(me_h + 1, n_h - 1), me_g)
    back_h = (tm, jnp.maximum(me_h - 1, 0), me_g)
    ahead_tm = (jnp.minimum(tm + 1, n_tm - 1), me_h, me_g)
    back_tm = (jnp.maximum(tm - 1, 0), me_h, me_g)

    def lanes(i, size):
        return pl.ds(pl.multiple_of(i * size, 128), size)

    def halo(part, way):
        cols = pl.ds(firsts[part] * HEAD, parts[part] * HEAD)
        src, dst, to = {
            0: (kv.at[:, 1:3, 2, :, cols], kv.at[:, 1:3, 0, :, cols], ahead_h),
            1: (kv.at[:, 1:3, 1, :, cols], kv.at[:, 1:3, 3, :, cols], back_h),
            2: (kv.at[:, 2, 1:3, :, cols], kv.at[:, 0, 1:3, :, cols], ahead_tm),
            3: (kv.at[:, 1, 1:3, :, cols], kv.at[:, 3, 1:3, :, cols], back_tm),
            4: (kv.at[:, 2, 0, :, cols], kv.at[:, 0, 0, :, cols], ahead_tm),
            5: (kv.at[:, 1, 0, :, cols], kv.at[:, 3, 0, :, cols], back_tm),
            6: (kv.at[:, 2, 3, :, cols], kv.at[:, 0, 3, :, cols], ahead_tm),
            7: (kv.at[:, 1, 3, :, cols], kv.at[:, 3, 3, :, cols], back_tm),
            8: (kv.at[:, 2, 2, :, cols], kv.at[:, 0, 0, :, cols], (ahead_tm[0], ahead_h[1], me_g)),
            9: (kv.at[:, 1, 2, :, cols], kv.at[:, 3, 0, :, cols], (back_tm[0], ahead_h[1], me_g)),
            10: (kv.at[:, 2, 1, :, cols], kv.at[:, 0, 3, :, cols], (ahead_tm[0], back_h[1], me_g)),
            11: (kv.at[:, 1, 1, :, cols], kv.at[:, 3, 3, :, cols], (back_tm[0], back_h[1], me_g)),
        }[way]
        return pltpu.make_async_remote_copy(
            src_ref=src, dst_ref=dst, send_sem=halo_send.at[part, way], recv_sem=halo_recv.at[part, way],
            device_id=to, device_id_type=MESH,
        )

    not_first_tm, not_last_tm = tm > 0, tm < n_tm - 1
    not_first_h, not_last_h = me_h > 0, me_h < n_h - 1
    sends = {
        0: not_last_h, 1: not_first_h, 2: not_last_tm, 3: not_first_tm,
        4: not_first_h & not_last_tm, 5: not_first_h & not_first_tm,
        6: not_last_h & not_last_tm, 7: not_last_h & not_first_tm,
        8: not_last_h & not_last_tm, 9: not_last_h & not_first_tm,
        10: not_first_h & not_last_tm, 11: not_first_h & not_first_tm,
    }
    receives = {
        0: not_first_h, 1: not_last_h, 2: not_first_tm, 3: not_last_tm,
        4: not_first_h & not_first_tm, 5: not_first_h & not_last_tm,
        6: not_last_h & not_first_tm, 7: not_last_h & not_last_tm,
        8: not_first_h & not_first_tm, 9: not_first_h & not_last_tm,
        10: not_last_h & not_first_tm, 11: not_last_h & not_last_tm,
    }

    def when_each(table, ways, part, act):
        for way in ways:
            @pl.when(table[way])
            def _(way=way):
                act(halo(part, way))

    def first_ways(part):
        return (0, 1, 2, 3) + ((8, 9, 10, 11) if part == n_parts - 1 else ())

    def second_ways(part):
        return () if part == n_parts - 1 else (4, 5, 6, 7)

    def late_ways(part):
        return (2, 3) + (second_ways(part) or (8, 9, 10, 11))

    def leave():
        for part in range(n_parts):
            when_each(sends, first_ways(part) + second_ways(part), part, lambda copy: copy.wait_send())

    my_rows = pl.ds(pl.multiple_of(core * HALF, 16), HALF)

    def gather_z(i):
        src = gath.at[me_h, my_rows]
        to = (tm, me_x * n_z + lax.rem(me_z + i, n_z), me_g)
        return pltpu.make_async_remote_copy(
            src_ref=src, dst_ref=src, send_sem=g_send.at[i], recv_sem=g_recv.at[0],
            device_id=to, device_id_type=MESH,
        )

    def gather_x(i):
        src = gath.at[pl.ds(me_x * n_z, n_z), my_rows]
        to = (tm, lax.rem(me_x + i, n_x) * n_z + me_z, me_g)
        return pltpu.make_async_remote_copy(
            src_ref=src, dst_ref=src, send_sem=g_send.at[n_z + i], recv_sem=g_recv.at[1],
            device_id=to, device_id_type=MESH,
        )

    def gather_core():
        src = gath.at[:, my_rows]
        return pltpu.make_async_remote_copy(
            src_ref=src, dst_ref=src, send_sem=g_send.at[0], recv_sem=g_recv.at[2],
            device_id=(2 * z_lo + 1 - core, me_h, me_g), device_id_type=MESH,
        )

    for i in range(1, n_z):
        gather_z(i).start()

    for part in range(n_parts):
        when_each(sends, first_ways(part), part, lambda copy: copy.start())
    for i in later_loads:
        loads[i].start()

    tokens = 4 * COLS
    q_at = lax.broadcasted_iota(jnp.int32, (tokens, 128), 0)
    feature = lax.broadcasted_iota(jnp.int32, (tokens, 128), 1)
    q_frame, q_row, q_tile = q_at // 64, lax.rem(q_at // 32, 2), lax.rem(q_at, 32) // TILE_W
    frame_at = tm * 2 - 1 + feature
    row_at = me_h * 2 - 1 + (feature - 4)
    gap_frame = jnp.where(
        (frame_at >= 0) & (frame_at < 2 * n_tm), jnp.abs(q_frame + 1 - feature), 99
    )
    gap_row = jnp.where(
        (row_at >= 0) & (row_at < 2 * n_h), jnp.abs(q_row + 1 - (feature - 4)), 99
    )
    gap_tile = jnp.abs(q_tile - (feature - 8))
    gap = jnp.where(
        feature < 4, gap_frame,
        jnp.where(feature < 8, gap_row, jnp.where(feature < 12, gap_tile, -1)),
    )
    k_at = lax.broadcasted_iota(jnp.int32, (512, 128), 0)
    k_feature = lax.broadcasted_iota(jnp.int32, (512, 128), 1)
    k_one_hot = (
        (k_feature == k_at // 128)
        | (k_feature == 4 + lax.rem(k_at // 32, 4))
        | (k_feature == 8 + lax.rem(k_at, 32) // TILE_W)
    ).astype(F32).astype(BF16)
    ones = jnp.ones((512, 128), BF16)
    factor = HEAD**-0.5 * math.log2(math.e)

    def attend(part):
        for head in range(firsts[part], firsts[part + 1]):
            cols = pl.ds(head * HEAD, HEAD)
            reach = jnp.where(
                lane < 4, win[0, head], jnp.where(lane < 8, win[1, head], win[2, head])
            )
            penalty = jnp.where(gap > reach, -FAR, 0.0).astype(BF16)
            query = jnp.concatenate([q[:, :, :, cols].reshape(tokens, HEAD), penalty], axis=1)
            key = jnp.concatenate([kv[0, :, :, :, cols].reshape(512, HEAD), k_one_hot], axis=1)
            scores = dot(query, key, 1, 1)
            top = jnp.max(scores, axis=1, keepdims=True)
            terms = jnp.exp2((scores - top) * factor).astype(BF16)
            value = jnp.concatenate([kv[1, :, :, :, cols].reshape(512, HEAD), ones], axis=1)
            mixed = dot(terms, value, 1, 0)
            att[:, cols] = (mixed[:, :HEAD] / mixed[:, HEAD:]).astype(BF16)

    step = 2 * UP_SHARD
    n_pairs = model // step

    def unrolled(carry, act):
        for i in range(n_pairs):
            carry = act(i, pl.ds(i * step, step), carry)
        return carry

    def sweep(carry, act):
        return lax.fori_loop(0, n_pairs, lambda i, c: act(i, lanes(i, step), c), carry)

    def fold(x):
        total = x[:, 0:128]
        for i in range(1, x.shape[1] // 128):
            total = total + x[:, i * 128 : (i + 1) * 128]
        return total

    def mean(total):
        return jnp.sum(total, axis=1, keepdims=True) * (1.0 / model)

    def prepare():
        def sums(_, cols, carry):
            sum_s, sum_w, sum_c = carry
            wide = w_t[:, cols].astype(F32)
            return (
                sum_s + fold(st[:, :, :, cols].reshape(tokens, step).astype(F32)),
                sum_w + fold(wide * (1.0 + mod[2, :, cols])),
                sum_c + fold(wide * mod[1, :, cols]),
            )

        narrow = jnp.zeros((LAT, 128), F32)
        sum_s, sum_w, sum_c = sweep((jnp.zeros((tokens, 128), F32), narrow, narrow), sums)
        mean_s, mean_w = mean(sum_s), mean(sum_w)

        def centre(_, cols, carry):
            even[:, cols] = st[:, :, :, cols].reshape(tokens, step).astype(F32) - mean_s
            rhs[0:64, cols] = (w_t[:, cols].astype(F32) * (1.0 + mod[2, :, cols]) - mean_w).astype(BF16)
            return carry

        sweep(0, centre)
        constant = jnp.sum(sum_c, axis=1, keepdims=True)
        shift = jnp.sum(jnp.where(unit_row == unit_lane, constant, 0.0), axis=0, keepdims=True)
        offset[...] = shift + jnp.concatenate([bias[...], jnp.zeros((1, 64), F32)], axis=1)

    def prepare_up():
        sum_b = sweep(
            jnp.zeros((RANK, 128), F32),
            lambda _, cols, total: total + fold(b_full[:, cols].astype(F32) * mod[0, :, cols]),
        )
        mean_b = mean(sum_b)

        def centre(_, cols, product):
            scaled = (b_full[:, cols].astype(F32) * mod[0, :, cols] - mean_b).astype(BF16)
            rhs[64:128, cols] = scaled
            return product + dot(rhs[0:64, cols], scaled, 1, 1)

        cross[:, 0:RANK] = sweep(jnp.zeros((LAT, RANK), F32), centre).astype(BF16)


    last_cols = firsts[-2] * HEAD

    def spread_x():
        for i in range(1, n_z):
            gather_z(i).wait_send()
        taken = gath.at[pl.ds(0, n_z - 1), my_rows]
        pltpu.make_async_copy(taken, taken, g_recv.at[0]).wait()
        for i in range(1, n_x):
            gather_x(i).start()

    def spread_core():
        for i in range(1, n_x):
            gather_x(i).wait_send()
        taken = gath.at[pl.ds(0, (n_x - 1) * n_z), my_rows]
        pltpu.make_async_copy(taken, taken, g_recv.at[1]).wait()
        pl.semaphore_signal(across, inc=1, device_id=(lax.rem(tm + 2, n_tm), me_h, me_g), device_id_type=MESH)
        gather_core().start()

    def lay_out():
        gather_core().wait()

        def adapter(pair, _):
            for i in range(2):
                both = gath[2 * pair + i, 96:144, :]
                at = pl.multiple_of((2 * pair + i) * 96, 16)
                a_full[pl.ds(at, 48), :] = both
                a_full[pl.ds(at + 48, 48), 0:64] = both[:, 64:128]
            at = pl.multiple_of(pair * step, 128)
            b_full[:, pl.ds(at, 128)] = gath[2 * pair, 0:64, :]
            b_full[:, pl.ds(at + 256, 128)] = gath[2 * pair + 1, 0:64, :]
            first = gath[2 * pair, 64:96, :].astype(F32)
            second = gath[2 * pair + 1, 64:96, :].astype(F32)
            b_full[0:32, pl.ds(at + 128, 128)] = jnp.where(
                left, first, pltpu.roll(second, 64, 1)
            ).astype(BF16)
            b_full[32:64, pl.ds(at + 128, 128)] = jnp.where(
                left, pltpu.roll(first, 64, 1), second
            ).astype(BF16)
            return 0

        lax.fori_loop(0, half_h, adapter, 0)
        prepare_up()

    def differ():
        for i in later_loads:
            if i not in (2, 7):
                loads[i].wait()
        for f in range(2):
            for j in range(16):
                cols = pl.ds(j * 128, 128)
                d2[pl.ds(f * 32 + 2 * j, 2), :] = nxt[0, f, :, cols] - lat[0, f, :, cols]
        for f in range(2):
            for r in range(2):
                pair = d2[pl.ds(f * 32 + r, 16, stride=2), :]
                dn[pl.ds(f * 64 + r * 32, 16, stride=2), :] = pair
                dn[pl.ds(f * 64 + r * 32 + 1, 16, stride=2), :] = pltpu.roll(pair, 64, 1)

    def arrive(part):
        when_each(receives, (0, 1), part, lambda copy: copy.wait_recv())
        when_each(sends, second_ways(part), part, lambda copy: copy.start())

    def finish_part(part):
        when_each(receives, late_ways(part), part, lambda copy: copy.wait_recv())
        attend(part)

    for i in (2, 7):
        loads[i].wait()
    differ()
    prepare()
    arrive(0)
    spread_x()
    arrive(1)
    spread_core()
    arrive(2)
    lay_out()
    for part in range(n_parts - 1):
        finish_part(part)
    low_sum = dot(att[:, 0:last_cols], a_full[0:last_cols, 0:64], 1, 0)
    arrive(n_parts - 1)
    finish_part(n_parts - 1)
    low = (low_sum + dot(att[:, last_cols:width], a_full[last_cols:width, 0:64], 1, 0)).astype(BF16)

    def forward(_, cols, carry):
        total, seen = carry
        apart = even[:, cols] + dot(low, rhs[64:128, cols], 1, 0)
        narrow = apart.astype(BF16)
        rhs[128:256, cols] = narrow
        return total + fold(apart * apart), seen + dot(narrow, rhs[0:128, cols], 1, 1)

    blank = jnp.zeros((tokens, 128), F32)
    total, seen = unrolled((blank, blank), forward)
    inverse = lax.rsqrt(mean(total) + NORM_EPS)
    by_weight = jnp.where(left, inverse * seen, 0.0)
    by_up = pltpu.roll(seen, 64, 1)[:, 0:64]
    residue = jnp.where(left, dn[...] - SAMPLER_STEP * (by_weight + offset[...]), 0.0)

    square = jnp.sum(jnp.sum(residue * residue, axis=0, keepdims=True), axis=1, keepdims=True)
    part_core[core] = jnp.broadcast_to(square, (8, 128))
    partner = (2 * z_lo + 1 - core, me_h, me_g)

    def sum_core():
        return pltpu.make_async_remote_copy(
            src_ref=part_core.at[core], dst_ref=part_core.at[core], send_sem=s_send.at[0], recv_sem=s_recv.at[0],
            device_id=partner, device_id_type=MESH,
        )

    sum_core().start()

    g_velocity = SAMPLER_STEP * residue
    along = inverse * (jnp.sum(g_velocity * by_weight, axis=1, keepdims=True) * (1.0 / model))
    by_token = (-(inverse * along) * low.astype(F32)).T.astype(BF16)
    by_lat = dot(low, (inverse * g_velocity).astype(BF16), 0, 0).astype(BF16)
    lhs = jnp.concatenate([by_lat, by_token], axis=1)

    def share_up(pair, cols, carry):
        up = mod[0, :, cols] * dot(lhs, rhs[:, cols], 1, 0)
        pack[pair, 0, 0:64, :] = up[:, 0:128].astype(BF16)
        pack[pair, 1, 0:64, :] = up[:, 256:384].astype(BF16)
        shared = up[:, 128:256]
        turned = pltpu.roll(shared, 64, 1)
        pack[pair, 0, 64:96, :] = jnp.where(left, shared[0:32], turned[32:64]).astype(BF16)
        pack[pair, 1, 64:96, :] = jnp.where(left, turned[0:32], shared[32:64]).astype(BF16)
        return carry

    unrolled(0, share_up)

    def to_mate(i):
        rows = (pl.ds(0, 96), pl.ds(96, 48))[i]
        return pltpu.make_async_remote_copy(
            src_ref=pack.at[:, 1 - core, rows], dst_ref=mate.at[:, rows],
            send_sem=r_send.at[i], recv_sem=r_recv.at[i], device_id=partner, device_id_type=MESH,
        )

    to_mate(0).start()
    g_low = inverse * (dot(g_velocity[:, 0:64].astype(BF16), cross[:, 0:RANK], 1, 0) - along * by_up)
    g_low_twice = jnp.concatenate([g_low, g_low], axis=1).astype(BF16)

    def share_down(pair, _):
        down = dot(att[:, pl.ds(pl.multiple_of(pair * 384, 128), 384)], g_low_twice, 0, 0)
        for i in range(4):
            top, low_end = down[i * 96 : i * 96 + 48], down[i * 96 + 48 : i * 96 + 96]
            pack[2 * pair + i // 2, i % 2, 96:144, :] = jnp.where(left, top, low_end).astype(BF16)
        return 0

    lax.fori_loop(0, half_h // 2, share_down, 0)
    to_mate(1).start()

    def add_mate(i):
        to_mate(i).wait()
        rows = (pl.ds(0, 96), pl.ds(96, 48))[i]

        def add(j, _):
            chip[j, rows, :] = (
                pack[j, core, rows, :].astype(F32) + mate[j, rows, :].astype(F32)
            ).astype(BF16)
            return 0

        lax.fori_loop(0, half_h, add, 0)

    takes = lax.rem(me_h, 2) == core
    slot = me_h * 2 + z_lo
    part_rows = (pl.ds(0, HALF), pl.ds(HALF, PIECE - HALF))

    def to_owner(i, zl):
        j = lax.rem(me_h // 2 + i, half_h)
        size = (HALF, PIECE - HALF)[zl]
        return pltpu.make_async_remote_copy(
            src_ref=chip.at[j, part_rows[zl]], dst_ref=got.at[slot, pl.ds(0, size)],
            send_sem=r_send.at[2 + 2 * i + zl], recv_sem=r_recv.at[2],
            device_id=(2 * zl + core, 2 * j + core, me_g), device_id_type=MESH,
        )

    def sum_owner(i, zl):
        j = lax.rem(me_h // 2 + i, half_h)
        return pltpu.make_async_remote_copy(
            src_ref=part_plane.at[slot], dst_ref=part_plane.at[slot], send_sem=s_send.at[1 + 2 * i + zl],
            recv_sem=s_recv.at[1], device_id=(2 * zl + core, 2 * j + core, me_g), device_id_type=MESH,
        )

    def for_owners(zl, act):
        @pl.when(jnp.logical_not(takes & (z_lo == zl)))
        def _():
            act(0, zl)

        for i in range(1, half_h):
            act(i, zl)

    pl.semaphore_wait(across, 1)
    sum_core().wait()
    part_plane[slot] = part_core[0] + part_core[1]
    for zl in range(2):
        for_owners(zl, lambda i, zl: sum_owner(i, zl).start())

    for zl in range(2):
        add_mate(zl)
        own = takes & (z_lo == zl)

        @pl.when(own)
        def _(zl=zl):
            size = (HALF, PIECE - HALF)[zl]
            got[slot, 0:size, :] = chip[me_h // 2, part_rows[zl], :]

        for_owners(zl, lambda i, zl: to_owner(i, zl).start())

    def to_group(i):
        return pltpu.make_async_remote_copy(
            src_ref=ysum.at[me_g], dst_ref=ysum.at[me_g], send_sem=r_send.at[2 + n_h + i], recv_sem=r_recv.at[3],
            device_id=(tm, me_h, lax.rem(me_g + i, n_g)), device_id_type=MESH,
        )

    def to_tm(i):
        there = lax.rem(tm + i, n_tm)
        return pltpu.make_async_remote_copy(
            src_ref=final.at[z_lo], dst_ref=final.at[z_lo], send_sem=r_send.at[2 + n_h + n_g + i],
            recv_sem=r_recv.at[4 + z_lo], device_id=(there, me_h, me_g), device_id_type=MESH,
        )

    @pl.when(takes)
    def _():
        arrived = part_plane.at[0 : plane - 1]
        pltpu.make_async_copy(arrived, arrived, s_recv.at[1]).wait()
        square = part_plane[0]
        for i in range(1, plane):
            square = square + part_plane[i]
        square = square[0:1, :]
        count = 4 * COLS * LAT * n_tm * n_h
        logp = -square / (2.0 * count) - HALF_LOG_TAU
        gain = adv[0]
        ratio = jnp.exp(logp - slp[0])
        low_end, high_end = 1.0 - CLIP_RANGE, 1.0 + CLIP_RANGE
        plain = -gain * ratio
        cut = -gain * jnp.clip(ratio, low_end, high_end)
        inside = jnp.where(
            (ratio > low_end) & (ratio < high_end), 1.0,
            jnp.where((ratio == low_end) | (ratio == high_end), 0.5, 0.0),
        )
        weight = jnp.where(plain > cut, 1.0, jnp.where(plain == cut, 0.5 + 0.5 * inside, inside))
        slope = weight * plain * (1.0 / n_g)

        for zl in range(2):
            @pl.when(z_lo == zl)
            def _(zl=zl):
                arrived = got.at[0 : plane - 1, pl.ds(0, (HALF, PIECE - HALF)[zl])]
                pltpu.make_async_copy(arrived, arrived, r_recv.at[2]).wait()
        share = lax.fori_loop(
            0, plane // 4,
            lambda i, sofar: sofar
            + ((got[4 * i].astype(F32) + got[4 * i + 1].astype(F32))
               + (got[4 * i + 2].astype(F32) + got[4 * i + 3].astype(F32))),
            jnp.zeros((HALF, 128), F32),
        )
        ysum[me_g] = (share * slope).astype(BF16)
        for i in range(1, n_g):
            to_group(i).start()
        pltpu.make_async_copy(ysum.at[0 : n_g - 1], ysum.at[0 : n_g - 1], r_recv.at[3]).wait()
        share = ysum[0].astype(F32)
        for i in range(1, n_g):
            share = share + ysum[i].astype(F32)
        final[z_lo] = share
        for i in range(1, n_tm):
            to_tm(i).start()
        other = 1 - z_lo
        pltpu.make_async_copy(final.at[other], final.at[other], r_recv.at[4 + other]).wait()
        for i in range(1, n_g):
            to_group(i).wait_send()
        for i in range(1, n_tm):
            to_tm(i).wait_send()

    @pl.when(jnp.logical_not(takes))
    def _():
        for zl in range(2):
            pltpu.make_async_copy(final.at[zl], final.at[zl], r_recv.at[4 + zl]).wait()

    out[0:HALF, :] = final[0]
    out[HALF:PIECE, :] = final[1, 0 : PIECE - HALF, :]

    leave()
    for zl in range(2):
        for_owners(zl, lambda i, zl: (to_owner(i, zl).wait_send(), sum_owner(i, zl).wait_send()))


def unpack_kernel(packed, down_t, up):
    odd = lax.rem(lax.axis_index("height"), 2) == 1
    full = packed[0:64, :]
    rest = packed[64:96, :]
    narrow = jnp.concatenate([rest[:, 0:64], rest[:, 64:128]], axis=0)

    @pl.when(odd)
    def _():
        up[...] = jnp.concatenate([narrow, full], axis=1)

    @pl.when(jnp.logical_not(odd))
    def _():
        up[...] = jnp.concatenate([full, narrow], axis=1)

    down = packed[96:144, :]
    down = jnp.concatenate([down[:, 0:64], down[:, 64:128]], axis=0)
    down_t[...] = down.T


def body(
    queries, keys, values, window, adapter_down_factor, adapter_up_factor, stream, modulation,
    closing_weight, closing_bias, latent, next_latent_sample, sampling_log_probability, advantage,
):
    heads = window.shape[0]
    width = heads * HEAD
    model = stream.shape[-1]
    n_tm, n_h, n_g = lax.axis_size("tm"), lax.axis_size("height"), lax.axis_size("group")
    n_z = 4 if n_h == 16 else 2
    parts = (4, 4, 3, 1) if heads == 12 else (1,) * heads
    dims = (n_tm, n_h, n_g, n_z, heads, parts)
    n_parts = len(parts)
    tokens = 4 * COLS
    vmem = pl.BlockSpec(memory_space=pltpu.VMEM)
    hbm = pl.BlockSpec(memory_space=pl.ANY)
    dma = pltpu.SemaphoreType.DMA
    packed = pl.pallas_call(
        functools.partial(kernel, dims),
        out_shape=jax.ShapeDtypeStruct((PIECE, 128), F32),
        in_specs=[hbm] * 14,
        out_specs=vmem,
        scratch_shapes=[
            pltpu.SMEM((3, heads), jnp.int32),
            pltpu.SMEM((1,), F32),
            pltpu.SMEM((1,), F32),
            pltpu.VMEM((RANK, DOWN_SHARD), BF16),
            pltpu.VMEM((RANK, UP_SHARD), BF16),
            pltpu.VMEM((3, 1, model), F32),
            pltpu.VMEM((1, LAT), F32),
            pltpu.VMEM((1, 2, 2, COLS * LAT), F32),
            pltpu.VMEM((1, 2, 2, COLS * LAT), F32),
            pltpu.VMEM((2, 2, COLS, width), BF16),
            pltpu.VMEM((2, 4, 4, COLS, width), BF16),
            pltpu.VMEM((2, 2, COLS, model), BF16),
            pltpu.VMEM((LAT, model), BF16),
            pltpu.VMEM((n_h, 2 * HALF, 128), BF16),
            pltpu.VMEM((width, 128), BF16),
            pltpu.VMEM((RANK, model), BF16),
            pltpu.VMEM((tokens, width), BF16),
            pltpu.VMEM((tokens, model), F32),
            pltpu.VMEM((256, model), BF16),
            pltpu.VMEM((n_h // 2, 2, PIECE, 128), BF16),
            pltpu.VMEM((n_h // 2, PIECE, 128), BF16),
            pltpu.VMEM((n_h // 2, PIECE, 128), BF16),
            pltpu.VMEM((2 * n_h, HALF, 128), BF16),
            pltpu.VMEM((n_g, HALF, 128), BF16),
            pltpu.VMEM((2, HALF, 128), F32),
            pltpu.VMEM((64, 128), F32),
            pltpu.VMEM((128, 128), F32),
            pltpu.VMEM((LAT, 128), BF16),
            pltpu.VMEM((1, 128), F32),
            pltpu.VMEM((2, 8, 128), F32),
            pltpu.VMEM((2 * n_h, 8, 128), F32),
            dma((14,)),
            dma((n_parts, 12)),
            dma((n_parts, 12)),
            dma((n_h,)),
            dma((3,)),
            dma((1 + n_h,)),
            dma((2,)),
            dma((2 + n_h + n_g + n_tm,)),
            dma((6,)),
            pltpu.SemaphoreType.REGULAR,
        ],
        compiler_params=pltpu.CompilerParams(
            collective_id=0, has_side_effects=True, vmem_limit_bytes=63 * 1024 * 1024
        ),
        name="step",
    )(
        queries, keys, values, window.T, adapter_down_factor.T, adapter_up_factor, stream,
        modulation.transpose(1, 0, 2), closing_weight.T, closing_bias.reshape(1, LAT), latent,
        next_latent_sample, sampling_log_probability, advantage,
    )
    down_t, up = pl.pallas_call(
        unpack_kernel,
        out_shape=(
            jax.ShapeDtypeStruct((RANK, DOWN_SHARD), F32),
            jax.ShapeDtypeStruct((RANK, UP_SHARD), F32),
        ),
        in_specs=[vmem],
        out_specs=(vmem, vmem),
        name="unpack",
    )(packed)
    return (down_t.T, up)


def solution(mesh):
    return jax.shard_map(
        body,
        mesh=mesh,
        in_specs=(
            P("group", "tm", "height", None, None),
            P("group", "tm", "height", None, None),
            P("group", "tm", "height", None, None),
            P(),
            P("height", None),
            P(None, "height"),
            P("group", "tm", "height", None, None),
            P("group", None, None),
            P(),
            P(),
            P("group", "tm", "height", None),
            P("group", "tm", "height", None),
            P("group"),
            P("group"),
        ),
        out_specs=(P("height", None), P(None, "height")),
        check_vma=False,
    )
```

```python
import functools
import math

import jax
import jax.numpy as jnp
from jax import lax
from jax.experimental import pallas as pl
from jax.experimental.pallas import tpu as pltpu
from jax.sharding import PartitionSpec as P

TILE_W = 8
COLS = 32
HEAD = 128
RANK = 64
LAT = 64
SAMPLER_STEP = -0.5
CLIP_RANGE = 0.2
NORM_EPS = 1e-06
HALF_LOG_TAU = 0.5 * math.log(2.0 * math.pi)
DOWN_SHARD = 96
UP_SHARD = 192
PIECE = 144
HALF = 80
FAR = 32768.0
F32 = jnp.float32
BF16 = jnp.bfloat16
MESH = pl.DeviceIdType.MESH


def dot(a, b, ca, cb):
    return lax.dot_general(a, b, (((ca,), (cb,)), ((), ())), preferred_element_type=F32)


def kernel(
    dims,
    q_hbm, k_hbm, v_hbm, win_hbm, a_hbm, b_hbm, st_hbm, mod_hbm, w_hbm, bias_hbm, lat_hbm, nxt_hbm,
    slp_hbm, adv_hbm,
    out,
    win, slp, adv, a_t, b_own, mod, bias, lat, nxt,
    q, kv, st, w_t, gath, a_full, b_full, att, even, rhs, pack, mate, chip, got, ysum, final,
    d2, dn, cross, offset, part_core, part_plane, load_sem, halo_send, halo_recv, g_send, g_recv, s_send, s_recv,
    r_send, r_recv, across,
):
    n_tm, n_h, n_g, n_z, heads, parts = dims
    width = heads * HEAD
    model = st.shape[-1]
    n_x = n_h // n_z
    tm, me_h, me_g = lax.axis_index("tm"), lax.axis_index("height"), lax.axis_index("group")
    core, z_lo = lax.rem(tm, 2), tm // 2
    me_x, me_z = me_h // n_z, lax.rem(me_h, n_z)
    half_h = n_h // 2
    me_h_odd = lax.rem(me_h, 2) == 1

    loads = [
        pltpu.make_async_copy(k_hbm.at[0], kv.at[0, 1:3, 1:3], load_sem.at[0]),
        pltpu.make_async_copy(v_hbm.at[0], kv.at[1, 1:3, 1:3], load_sem.at[1]),
        pltpu.make_async_copy(q_hbm.at[0], q, load_sem.at[2]),
        pltpu.make_async_copy(st_hbm.at[0], st, load_sem.at[3]),
        pltpu.make_async_copy(w_hbm, w_t, load_sem.at[4]),
    ]
    small = ((a_hbm, a_t), (b_hbm, b_own), (win_hbm, win), (mod_hbm, mod), (bias_hbm, bias), (lat_hbm, lat),
             (nxt_hbm, nxt), (slp_hbm, slp), (adv_hbm, adv))
    loads += [pltpu.make_async_copy(*ends, load_sem.at[5 + i]) for i, ends in enumerate(small)]
    first_loads, later_loads = (0, 1, 5, 6), (2, 3, 4, 7, 8, 9, 10, 11, 12, 13)
    for i in first_loads:
        loads[i].start()

    barrier = pltpu.get_barrier_semaphore()
    plane = 2 * n_h

    def greet(height, at_tm):
        pl.semaphore_signal(barrier, inc=1, device_id=(at_tm, height, me_g), device_id_type=MESH)

    for i in range(1, n_z):
        greet(me_x * n_z + lax.rem(me_z + i, n_z), tm)
    for i in range(1, n_x):
        greet(lax.rem(me_x + i, n_x) * n_z + me_z, tm)
    greet(me_h, lax.rem(tm + 2, n_tm))
    crosses = (me_z == n_z - 1, me_z == 0)

    @pl.when(crosses[0])
    def _():
        greet(lax.rem(me_h + 1, n_h), tm)

    @pl.when(crosses[1])
    def _():
        greet(lax.rem(me_h + n_h - 1, n_h), tm)


    def greet_group(i, _):
        pl.semaphore_signal(
            barrier, inc=1, device_id=(tm, me_h, lax.rem(me_g + i, n_g)), device_id_type=MESH
        )
        return 0

    lax.fori_loop(1, n_g, greet_group, 0)
    for zl in range(2):
        pl.semaphore_signal(
            barrier, inc=1, device_id=(2 * zl + 1 - core, me_h, me_g), device_id_type=MESH
        )
        for step_h in (1, n_h - 1):
            pl.semaphore_signal(
                barrier, inc=1, device_id=(2 * zl + 1 - core, lax.rem(me_h + step_h, n_h), me_g),
                device_id_type=MESH,
            )

    lane = lax.broadcasted_iota(jnp.int32, (1, 128), 1)
    left = lane < 64
    unit_row = lax.broadcasted_iota(jnp.int32, (64, 128), 0)
    unit_lane = lax.broadcasted_iota(jnp.int32, (64, 128), 1)
    loads[5].wait()
    loads[6].wait()
    twice = (lax.rem(unit_lane, 64) == unit_row).astype(F32).astype(BF16)
    a_rows = dot(a_t[...], twice, 0, 0)
    b_wide = b_own[...].astype(F32)
    b_even, b_odd = b_wide[:, 0:128], b_wide[:, 64:192]
    edge = jnp.where(me_h_odd, b_wide[:, 0:64], b_wide[:, 128:192])
    own_rows = jnp.concatenate(
        [
            jnp.where(me_h_odd, b_odd, b_even),
            jnp.concatenate([edge[0:32], edge[32:64]], axis=1),
            jnp.where(left, a_rows[0:48], a_rows[48:96]),
        ],
        axis=0,
    ).astype(BF16)

    @pl.when(core == 0)
    def _():
        gath[me_h, 0:HALF, :] = own_rows[0:HALF]

    @pl.when(core == 1)
    def _():
        gath[me_h, HALF:PIECE, :] = own_rows[HALF:PIECE]

    first_tm, last_tm = tm == 0, tm == n_tm - 1
    first_h, last_h = me_h == 0, me_h == n_h - 1

    @pl.when(first_tm)
    def _():
        kv[:, 0:1] = jnp.zeros((2, 1, 4, COLS, width), BF16)

    @pl.when(last_tm)
    def _():
        kv[:, 3:4] = jnp.zeros((2, 1, 4, COLS, width), BF16)

    @pl.when(first_h)
    def _():
        kv[:, :, 0:1] = jnp.zeros((2, 4, 1, COLS, width), BF16)

    @pl.when(last_h)
    def _():
        kv[:, :, 3:4] = jnp.zeros((2, 4, 1, COLS, width), BF16)

    loads[0].wait()
    loads[1].wait()
    crossing = crosses[0].astype(jnp.int32) + crosses[1].astype(jnp.int32)
    pl.semaphore_wait(barrier, n_z - 1 + n_x - 1 + 1 + n_g - 1 + 6 + crossing)

    n_parts = len(parts)
    firsts = [sum(parts[:i]) for i in range(n_parts + 1)]
    ahead_h = (tm, jnp.minimum(me_h + 1, n_h - 1), me_g)
    back_h = (tm, jnp.maximum(me_h - 1, 0), me_g)
    ahead_tm = (jnp.minimum(tm + 1, n_tm - 1), me_h, me_g)
    back_tm = (jnp.maximum(tm - 1, 0), me_h, me_g)

    def lanes(i, size):
        return pl.ds(pl.multiple_of(i * size, 128), size)

    def halo(part, way):
        cols = pl.ds(firsts[part] * HEAD, parts[part] * HEAD)
        src, dst, to = {
            0: (kv.at[:, 1:3, 2, :, cols], kv.at[:, 1:3, 0, :, cols], ahead_h),
            1: (kv.at[:, 1:3, 1, :, cols], kv.at[:, 1:3, 3, :, cols], back_h),
            2: (kv.at[:, 2, 1:3, :, cols], kv.at[:, 0, 1:3, :, cols], ahead_tm),
            3: (kv.at[:, 1, 1:3, :, cols], kv.at[:, 3, 1:3, :, cols], back_tm),
            4: (kv.at[:, 2, 0, :, cols], kv.at[:, 0, 0, :, cols], ahead_tm),
            5: (kv.at[:, 1, 0, :, cols], kv.at[:, 3, 0, :, cols], back_tm),
            6: (kv.at[:, 2, 3, :, cols], kv.at[:, 0, 3, :, cols], ahead_tm),
            7: (kv.at[:, 1, 3, :, cols], kv.at[:, 3, 3, :, cols], back_tm),
            8: (kv.at[:, 2, 2, :, cols], kv.at[:, 0, 0, :, cols], (ahead_tm[0], ahead_h[1], me_g)),
            9: (kv.at[:, 1, 2, :, cols], kv.at[:, 3, 0, :, cols], (back_tm[0], ahead_h[1], me_g)),
            10: (kv.at[:, 2, 1, :, cols], kv.at[:, 0, 3, :, cols], (ahead_tm[0], back_h[1], me_g)),
            11: (kv.at[:, 1, 1, :, cols], kv.at[:, 3, 3, :, cols], (back_tm[0], back_h[1], me_g)),
        }[way]
        return pltpu.make_async_remote_copy(
            src_ref=src, dst_ref=dst, send_sem=halo_send.at[part, way], recv_sem=halo_recv.at[part, way],
            device_id=to, device_id_type=MESH,
        )

    not_first_tm, not_last_tm = tm > 0, tm < n_tm - 1
    not_first_h, not_last_h = me_h > 0, me_h < n_h - 1
    sends = {
        0: not_last_h, 1: not_first_h, 2: not_last_tm, 3: not_first_tm,
        4: not_first_h & not_last_tm, 5: not_first_h & not_first_tm,
        6: not_last_h & not_last_tm, 7: not_last_h & not_first_tm,
        8: not_last_h & not_last_tm, 9: not_last_h & not_first_tm,
        10: not_first_h & not_last_tm, 11: not_first_h & not_first_tm,
    }
    receives = {
        0: not_first_h, 1: not_last_h, 2: not_first_tm, 3: not_last_tm,
        4: not_first_h & not_first_tm, 5: not_first_h & not_last_tm,
        6: not_last_h & not_first_tm, 7: not_last_h & not_last_tm,
        8: not_first_h & not_first_tm, 9: not_first_h & not_last_tm,
        10: not_last_h & not_first_tm, 11: not_last_h & not_last_tm,
    }

    def when_each(table, ways, part, act):
        for way in ways:
            @pl.when(table[way])
            def _(way=way):
                act(halo(part, way))

    def first_ways(part):
        return (0, 1, 2, 3) + ((8, 9, 10, 11) if part == n_parts - 1 else ())

    def second_ways(part):
        return () if part == n_parts - 1 else (4, 5, 6, 7)

    def late_ways(part):
        return (2, 3) + (second_ways(part) or (8, 9, 10, 11))

    def leave():
        for part in range(n_parts):
            when_each(sends, first_ways(part) + second_ways(part), part, lambda copy: copy.wait_send())

    my_rows = pl.ds(pl.multiple_of(core * HALF, 16), HALF)

    def gather_z(i):
        src = gath.at[me_h, my_rows]
        to = (tm, me_x * n_z + lax.rem(me_z + i, n_z), me_g)
        return pltpu.make_async_remote_copy(
            src_ref=src, dst_ref=src, send_sem=g_send.at[i], recv_sem=g_recv.at[0],
            device_id=to, device_id_type=MESH,
        )

    def gather_x(i):
        src = gath.at[pl.ds(me_x * n_z, n_z), my_rows]
        to = (tm, lax.rem(me_x + i, n_x) * n_z + me_z, me_g)
        return pltpu.make_async_remote_copy(
            src_ref=src, dst_ref=src, send_sem=g_send.at[n_z + i], recv_sem=g_recv.at[1],
            device_id=to, device_id_type=MESH,
        )

    def gather_core():
        src = gath.at[:, my_rows]
        return pltpu.make_async_remote_copy(
            src_ref=src, dst_ref=src, send_sem=g_send.at[0], recv_sem=g_recv.at[2],
            device_id=(2 * z_lo + 1 - core, me_h, me_g), device_id_type=MESH,
        )

    for i in range(1, n_z):
        gather_z(i).start()

    for part in range(n_parts):
        when_each(sends, first_ways(part), part, lambda copy: copy.start())
    for i in later_loads:
        loads[i].start()

    tokens = 4 * COLS
    q_at = lax.broadcasted_iota(jnp.int32, (tokens, 128), 0)
    feature = lax.broadcasted_iota(jnp.int32, (tokens, 128), 1)
    q_frame, q_row, q_tile = q_at // 64, lax.rem(q_at // 32, 2), lax.rem(q_at, 32) // TILE_W
    frame_at = tm * 2 - 1 + feature
    row_at = me_h * 2 - 1 + (feature - 4)
    gap_frame = jnp.where(
        (frame_at >= 0) & (frame_at < 2 * n_tm), jnp.abs(q_frame + 1 - feature), 99
    )
    gap_row = jnp.where(
        (row_at >= 0) & (row_at < 2 * n_h), jnp.abs(q_row + 1 - (feature - 4)), 99
    )
    gap_tile = jnp.abs(q_tile - (feature - 8))
    gap = jnp.where(
        feature < 4, gap_frame,
        jnp.where(feature < 8, gap_row, jnp.where(feature < 12, gap_tile, -1)),
    )
    k_at = lax.broadcasted_iota(jnp.int32, (512, 128), 0)
    k_feature = lax.broadcasted_iota(jnp.int32, (512, 128), 1)
    k_one_hot = (
        (k_feature == k_at // 128)
        | (k_feature == 4 + lax.rem(k_at // 32, 4))
        | (k_feature == 8 + lax.rem(k_at, 32) // TILE_W)
    ).astype(F32).astype(BF16)
    ones = jnp.ones((512, 128), BF16)
    factor = HEAD**-0.5 * math.log2(math.e)

    def attend(part):
        for head in range(firsts[part], firsts[part + 1]):
            cols = pl.ds(head * HEAD, HEAD)
            reach = jnp.where(
                lane < 4, win[0, head], jnp.where(lane < 8, win[1, head], win[2, head])
            )
            penalty = jnp.where(gap > reach, -FAR, 0.0).astype(BF16)
            query = jnp.concatenate([q[:, :, :, cols].reshape(tokens, HEAD), penalty], axis=1)
            key = jnp.concatenate([kv[0, :, :, :, cols].reshape(512, HEAD), k_one_hot], axis=1)
            scores = dot(query, key, 1, 1)
            top = jnp.max(scores, axis=1, keepdims=True)
            terms = jnp.exp2((scores - top) * factor).astype(BF16)
            value = jnp.concatenate([kv[1, :, :, :, cols].reshape(512, HEAD), ones], axis=1)
            mixed = dot(terms, value, 1, 0)
            att[:, cols] = (mixed[:, :HEAD] / mixed[:, HEAD:]).astype(BF16)

    step = 2 * UP_SHARD
    n_pairs = model // step

    def unrolled(carry, act):
        for i in range(n_pairs):
            carry = act(i, pl.ds(i * step, step), carry)
        return carry

    def sweep(carry, act):
        return lax.fori_loop(0, n_pairs, lambda i, c: act(i, lanes(i, step), c), carry)

    def fold(x):
        total = x[:, 0:128]
        for i in range(1, x.shape[1] // 128):
            total = total + x[:, i * 128 : (i + 1) * 128]
        return total

    def mean(total):
        return jnp.sum(total, axis=1, keepdims=True) * (1.0 / model)

    def prepare():
        def sums(_, cols, carry):
            sum_s, sum_w, sum_c = carry
            wide = w_t[:, cols].astype(F32)
            return (
                sum_s + fold(st[:, :, :, cols].reshape(tokens, step).astype(F32)),
                sum_w + fold(wide * (1.0 + mod[2, :, cols])),
                sum_c + fold(wide * mod[1, :, cols]),
            )

        narrow = jnp.zeros((LAT, 128), F32)
        sum_s, sum_w, sum_c = sweep((jnp.zeros((tokens, 128), F32), narrow, narrow), sums)
        mean_s, mean_w = mean(sum_s), mean(sum_w)

        def centre(_, cols, carry):
            even[:, cols] = st[:, :, :, cols].reshape(tokens, step).astype(F32) - mean_s
            rhs[0:64, cols] = (w_t[:, cols].astype(F32) * (1.0 + mod[2, :, cols]) - mean_w).astype(BF16)
            return carry

        sweep(0, centre)
        constant = jnp.sum(sum_c, axis=1, keepdims=True)
        shift = jnp.sum(jnp.where(unit_row == unit_lane, constant, 0.0), axis=0, keepdims=True)
        offset[...] = shift + jnp.concatenate([bias[...], jnp.zeros((1, 64), F32)], axis=1)

    def prepare_up():
        sum_b = sweep(
            jnp.zeros((RANK, 128), F32),
            lambda _, cols, total: total + fold(b_full[:, cols].astype(F32) * mod[0, :, cols]),
        )
        mean_b = mean(sum_b)

        def centre(_, cols, product):
            scaled = (b_full[:, cols].astype(F32) * mod[0, :, cols] - mean_b).astype(BF16)
            rhs[64:128, cols] = scaled
            return product + dot(rhs[0:64, cols], scaled, 1, 1)

        cross[:, 0:RANK] = sweep(jnp.zeros((LAT, RANK), F32), centre).astype(BF16)


    last_cols = firsts[-2] * HEAD

    def spread_x():
        for i in range(1, n_z):
            gather_z(i).wait_send()
        taken = gath.at[pl.ds(0, n_z - 1), my_rows]
        pltpu.make_async_copy(taken, taken, g_recv.at[0]).wait()
        for i in range(1, n_x):
            gather_x(i).start()

    def spread_core():
        for i in range(1, n_x):
            gather_x(i).wait_send()
        taken = gath.at[pl.ds(0, (n_x - 1) * n_z), my_rows]
        pltpu.make_async_copy(taken, taken, g_recv.at[1]).wait()
        pl.semaphore_signal(across, inc=1, device_id=(lax.rem(tm + 2, n_tm), me_h, me_g), device_id_type=MESH)
        gather_core().start()

    def lay_out():
        gather_core().wait()

        def adapter(pair, _):
            for i in range(2):
                both = gath[2 * pair + i, 96:144, :]
                at = pl.multiple_of((2 * pair + i) * 96, 16)
                a_full[pl.ds(at, 48), :] = both
                a_full[pl.ds(at + 48, 48), 0:64] = both[:, 64:128]
            at = pl.multiple_of(pair * step, 128)
            b_full[:, pl.ds(at, 128)] = gath[2 * pair, 0:64, :]
            b_full[:, pl.ds(at + 256, 128)] = gath[2 * pair + 1, 0:64, :]
            first = gath[2 * pair, 64:96, :].astype(F32)
            second = gath[2 * pair + 1, 64:96, :].astype(F32)
            b_full[0:32, pl.ds(at + 128, 128)] = jnp.where(
                left, first, pltpu.roll(second, 64, 1)
            ).astype(BF16)
            b_full[32:64, pl.ds(at + 128, 128)] = jnp.where(
                left, pltpu.roll(first, 64, 1), second
            ).astype(BF16)
            return 0

        lax.fori_loop(0, half_h, adapter, 0)
        prepare_up()

    def differ():
        for i in later_loads:
            if i not in (2, 7):
                loads[i].wait()
        for f in range(2):
            for j in range(16):
                cols = pl.ds(j * 128, 128)
                d2[pl.ds(f * 32 + 2 * j, 2), :] = nxt[0, f, :, cols] - lat[0, f, :, cols]
        for f in range(2):
            for r in range(2):
                pair = d2[pl.ds(f * 32 + r, 16, stride=2), :]
                dn[pl.ds(f * 64 + r * 32, 16, stride=2), :] = pair
                dn[pl.ds(f * 64 + r * 32 + 1, 16, stride=2), :] = pltpu.roll(pair, 64, 1)

    def arrive(part):
        when_each(receives, (0, 1), part, lambda copy: copy.wait_recv())
        when_each(sends, second_ways(part), part, lambda copy: copy.start())

    def finish_part(part):
        when_each(receives, late_ways(part), part, lambda copy: copy.wait_recv())
        attend(part)

    for i in (2, 7):
        loads[i].wait()
    differ()
    prepare()
    arrive(0)
    spread_x()
    arrive(1)
    spread_core()
    arrive(2)
    lay_out()
    for part in range(n_parts - 1):
        finish_part(part)
    low_sum = dot(att[:, 0:last_cols], a_full[0:last_cols, 0:64], 1, 0)
    arrive(n_parts - 1)
    finish_part(n_parts - 1)
    low = (low_sum + dot(att[:, last_cols:width], a_full[last_cols:width, 0:64], 1, 0)).astype(BF16)

    def forward(_, cols, carry):
        total, seen = carry
        apart = even[:, cols] + dot(low, rhs[64:128, cols], 1, 0)
        narrow = apart.astype(BF16)
        rhs[128:256, cols] = narrow
        return total + fold(apart * apart), seen + dot(narrow, rhs[0:128, cols], 1, 1)

    blank = jnp.zeros((tokens, 128), F32)
    total, seen = unrolled((blank, blank), forward)
    inverse = lax.rsqrt(mean(total) + NORM_EPS)
    by_weight = jnp.where(left, inverse * seen, 0.0)
    by_up = pltpu.roll(seen, 64, 1)[:, 0:64]
    residue = jnp.where(left, dn[...] - SAMPLER_STEP * (by_weight + offset[...]), 0.0)

    square = jnp.sum(jnp.sum(residue * residue, axis=0, keepdims=True), axis=1, keepdims=True)
    part_core[core] = jnp.broadcast_to(square, (8, 128))
    partner = (2 * z_lo + 1 - core, me_h, me_g)

    def sum_core():
        return pltpu.make_async_remote_copy(
            src_ref=part_core.at[core], dst_ref=part_core.at[core], send_sem=s_send.at[0], recv_sem=s_recv.at[0],
            device_id=partner, device_id_type=MESH,
        )

    sum_core().start()

    g_velocity = SAMPLER_STEP * residue
    along = inverse * (jnp.sum(g_velocity * by_weight, axis=1, keepdims=True) * (1.0 / model))
    by_token = (-(inverse * along) * low.astype(F32)).T.astype(BF16)
    by_lat = dot(low, (inverse * g_velocity).astype(BF16), 0, 0).astype(BF16)
    lhs = jnp.concatenate([by_lat, by_token], axis=1)

    def share_up(pair, cols, carry):
        up = mod[0, :, cols] * dot(lhs, rhs[:, cols], 1, 0)
        pack[pair, 0, 0:64, :] = up[:, 0:128].astype(BF16)
        pack[pair, 1, 0:64, :] = up[:, 256:384].astype(BF16)
        shared = up[:, 128:256]
        turned = pltpu.roll(shared, 64, 1)
        pack[pair, 0, 64:96, :] = jnp.where(left, shared[0:32], turned[32:64]).astype(BF16)
        pack[pair, 1, 64:96, :] = jnp.where(left, turned[0:32], shared[32:64]).astype(BF16)
        return carry

    unrolled(0, share_up)

    def to_mate(i):
        rows = (pl.ds(0, 96), pl.ds(96, 48))[i]
        return pltpu.make_async_remote_copy(
            src_ref=pack.at[:, 1 - core, rows], dst_ref=mate.at[:, rows],
            send_sem=r_send.at[i], recv_sem=r_recv.at[i], device_id=partner, device_id_type=MESH,
        )

    to_mate(0).start()
    g_low = inverse * (dot(g_velocity[:, 0:64].astype(BF16), cross[:, 0:RANK], 1, 0) - along * by_up)
    g_low_twice = jnp.concatenate([g_low, g_low], axis=1).astype(BF16)

    def share_down(pair, _):
        down = dot(att[:, pl.ds(pl.multiple_of(pair * 384, 128), 384)], g_low_twice, 0, 0)
        for i in range(4):
            top, low_end = down[i * 96 : i * 96 + 48], down[i * 96 + 48 : i * 96 + 96]
            pack[2 * pair + i // 2, i % 2, 96:144, :] = jnp.where(left, top, low_end).astype(BF16)
        return 0

    lax.fori_loop(0, half_h // 2, share_down, 0)
    to_mate(1).start()

    def add_mate(i):
        to_mate(i).wait()
        rows = (pl.ds(0, 96), pl.ds(96, 48))[i]

        def add(j, _):
            chip[j, rows, :] = (
                pack[j, core, rows, :].astype(F32) + mate[j, rows, :].astype(F32)
            ).astype(BF16)
            return 0

        lax.fori_loop(0, half_h, add, 0)

    takes = lax.rem(me_h, 2) == core
    slot = me_h * 2 + z_lo
    part_rows = (pl.ds(0, HALF), pl.ds(HALF, PIECE - HALF))

    def to_owner(i, zl):
        j = lax.rem(me_h // 2 + i, half_h)
        size = (HALF, PIECE - HALF)[zl]
        return pltpu.make_async_remote_copy(
            src_ref=chip.at[j, part_rows[zl]], dst_ref=got.at[slot, pl.ds(0, size)],
            send_sem=r_send.at[2 + 2 * i + zl], recv_sem=r_recv.at[2],
            device_id=(2 * zl + core, 2 * j + core, me_g), device_id_type=MESH,
        )

    def sum_owner(i, zl):
        j = lax.rem(me_h // 2 + i, half_h)
        return pltpu.make_async_remote_copy(
            src_ref=part_plane.at[slot], dst_ref=part_plane.at[slot], send_sem=s_send.at[1 + 2 * i + zl],
            recv_sem=s_recv.at[1], device_id=(2 * zl + core, 2 * j + core, me_g), device_id_type=MESH,
        )

    def for_owners(zl, act):
        @pl.when(jnp.logical_not(takes & (z_lo == zl)))
        def _():
            act(0, zl)

        for i in range(1, half_h):
            act(i, zl)

    pl.semaphore_wait(across, 1)
    sum_core().wait()
    part_plane[slot] = part_core[0] + part_core[1]
    for zl in range(2):
        for_owners(zl, lambda i, zl: sum_owner(i, zl).start())

    for zl in range(2):
        add_mate(zl)
        own = takes & (z_lo == zl)

        @pl.when(own)
        def _(zl=zl):
            size = (HALF, PIECE - HALF)[zl]
            got[slot, 0:size, :] = chip[me_h // 2, part_rows[zl], :]

        for_owners(zl, lambda i, zl: to_owner(i, zl).start())

    def to_group(i):
        return pltpu.make_async_remote_copy(
            src_ref=ysum.at[me_g], dst_ref=ysum.at[me_g], send_sem=r_send.at[2 + n_h + i], recv_sem=r_recv.at[3],
            device_id=(tm, me_h, lax.rem(me_g + i, n_g)), device_id_type=MESH,
        )

    def to_tm(i):
        there = lax.rem(tm + i, n_tm)
        return pltpu.make_async_remote_copy(
            src_ref=final.at[z_lo], dst_ref=final.at[z_lo], send_sem=r_send.at[2 + n_h + n_g + i],
            recv_sem=r_recv.at[4 + z_lo], device_id=(there, me_h, me_g), device_id_type=MESH,
        )

    @pl.when(takes)
    def _():
        arrived = part_plane.at[0 : plane - 1]
        pltpu.make_async_copy(arrived, arrived, s_recv.at[1]).wait()
        square = part_plane[0]
        for i in range(1, plane):
            square = square + part_plane[i]
        square = square[0:1, :]
        count = 4 * COLS * LAT * n_tm * n_h
        logp = -square / (2.0 * count) - HALF_LOG_TAU
        gain = adv[0]
        ratio = jnp.exp(logp - slp[0])
        low_end, high_end = 1.0 - CLIP_RANGE, 1.0 + CLIP_RANGE
        plain = -gain * ratio
        cut = -gain * jnp.clip(ratio, low_end, high_end)
        inside = jnp.where(
            (ratio > low_end) & (ratio < high_end), 1.0,
            jnp.where((ratio == low_end) | (ratio == high_end), 0.5, 0.0),
        )
        weight = jnp.where(plain > cut, 1.0, jnp.where(plain == cut, 0.5 + 0.5 * inside, inside))
        slope = weight * plain * (1.0 / n_g)

        for zl in range(2):
            @pl.when(z_lo == zl)
            def _(zl=zl):
                arrived = got.at[0 : plane - 1, pl.ds(0, (HALF, PIECE - HALF)[zl])]
                pltpu.make_async_copy(arrived, arrived, r_recv.at[2]).wait()
        share = lax.fori_loop(
            0, plane // 4,
            lambda i, sofar: sofar
            + ((got[4 * i].astype(F32) + got[4 * i + 1].astype(F32))
               + (got[4 * i + 2].astype(F32) + got[4 * i + 3].astype(F32))),
            jnp.zeros((HALF, 128), F32),
        )
        ysum[me_g] = (share * slope).astype(BF16)
        for i in range(1, n_g):
            to_group(i).start()
        pltpu.make_async_copy(ysum.at[0 : n_g - 1], ysum.at[0 : n_g - 1], r_recv.at[3]).wait()
        share = ysum[0].astype(F32)
        for i in range(1, n_g):
            share = share + ysum[i].astype(F32)
        final[z_lo] = share.astype(BF16)
        for i in range(1, n_tm):
            to_tm(i).start()
        other = 1 - z_lo
        pltpu.make_async_copy(final.at[other], final.at[other], r_recv.at[4 + other]).wait()
        for i in range(1, n_g):
            to_group(i).wait_send()
        for i in range(1, n_tm):
            to_tm(i).wait_send()

    @pl.when(jnp.logical_not(takes))
    def _():
        for zl in range(2):
            pltpu.make_async_copy(final.at[zl], final.at[zl], r_recv.at[4 + zl]).wait()

    out[0:HALF, :] = final[0].astype(F32)
    out[HALF:PIECE, :] = final[1, 0 : PIECE - HALF, :].astype(F32)

    leave()
    for zl in range(2):
        for_owners(zl, lambda i, zl: (to_owner(i, zl).wait_send(), sum_owner(i, zl).wait_send()))


def unpack_kernel(packed, down_t, up):
    odd = lax.rem(lax.axis_index("height"), 2) == 1
    full = packed[0:64, :]
    rest = packed[64:96, :]
    narrow = jnp.concatenate([rest[:, 0:64], rest[:, 64:128]], axis=0)

    @pl.when(odd)
    def _():
        up[...] = jnp.concatenate([narrow, full], axis=1)

    @pl.when(jnp.logical_not(odd))
    def _():
        up[...] = jnp.concatenate([full, narrow], axis=1)

    down = packed[96:144, :]
    down = jnp.concatenate([down[:, 0:64], down[:, 64:128]], axis=0)
    down_t[...] = down.T


def body(
    queries, keys, values, window, adapter_down_factor, adapter_up_factor, stream, modulation,
    closing_weight, closing_bias, latent, next_latent_sample, sampling_log_probability, advantage,
):
    heads = window.shape[0]
    width = heads * HEAD
    model = stream.shape[-1]
    n_tm, n_h, n_g = lax.axis_size("tm"), lax.axis_size("height"), lax.axis_size("group")
    n_z = 4 if n_h == 16 else 2
    parts = (4, 4, 3, 1) if heads == 12 else (1,) * heads
    dims = (n_tm, n_h, n_g, n_z, heads, parts)
    n_parts = len(parts)
    tokens = 4 * COLS
    vmem = pl.BlockSpec(memory_space=pltpu.VMEM)
    hbm = pl.BlockSpec(memory_space=pl.ANY)
    dma = pltpu.SemaphoreType.DMA
    packed = pl.pallas_call(
        functools.partial(kernel, dims),
        out_shape=jax.ShapeDtypeStruct((PIECE, 128), F32),
        in_specs=[hbm] * 14,
        out_specs=vmem,
        scratch_shapes=[
            pltpu.SMEM((3, heads), jnp.int32),
            pltpu.SMEM((1,), F32),
            pltpu.SMEM((1,), F32),
            pltpu.VMEM((RANK, DOWN_SHARD), BF16),
            pltpu.VMEM((RANK, UP_SHARD), BF16),
            pltpu.VMEM((3, 1, model), F32),
            pltpu.VMEM((1, LAT), F32),
            pltpu.VMEM((1, 2, 2, COLS * LAT), F32),
            pltpu.VMEM((1, 2, 2, COLS * LAT), F32),
            pltpu.VMEM((2, 2, COLS, width), BF16),
            pltpu.VMEM((2, 4, 4, COLS, width), BF16),
            pltpu.VMEM((2, 2, COLS, model), BF16),
            pltpu.VMEM((LAT, model), BF16),
            pltpu.VMEM((n_h, 2 * HALF, 128), BF16),
            pltpu.VMEM((width, 128), BF16),
            pltpu.VMEM((RANK, model), BF16),
            pltpu.VMEM((tokens, width), BF16),
            pltpu.VMEM((tokens, model), F32),
            pltpu.VMEM((256, model), BF16),
            pltpu.VMEM((n_h // 2, 2, PIECE, 128), BF16),
            pltpu.VMEM((n_h // 2, PIECE, 128), BF16),
            pltpu.VMEM((n_h // 2, PIECE, 128), BF16),
            pltpu.VMEM((2 * n_h, HALF, 128), BF16),
            pltpu.VMEM((n_g, HALF, 128), BF16),
            pltpu.VMEM((2, HALF, 128), BF16),
            pltpu.VMEM((64, 128), F32),
            pltpu.VMEM((128, 128), F32),
            pltpu.VMEM((LAT, 128), BF16),
            pltpu.VMEM((1, 128), F32),
            pltpu.VMEM((2, 8, 128), F32),
            pltpu.VMEM((2 * n_h, 8, 128), F32),
            dma((14,)),
            dma((n_parts, 12)),
            dma((n_parts, 12)),
            dma((n_h,)),
            dma((3,)),
            dma((1 + n_h,)),
            dma((2,)),
            dma((2 + n_h + n_g + n_tm,)),
            dma((6,)),
            pltpu.SemaphoreType.REGULAR,
        ],
        compiler_params=pltpu.CompilerParams(
            collective_id=0, has_side_effects=True, vmem_limit_bytes=63 * 1024 * 1024
        ),
        name="step",
    )(
        queries, keys, values, window.T, adapter_down_factor.T, adapter_up_factor, stream,
        modulation.transpose(1, 0, 2), closing_weight.T, closing_bias.reshape(1, LAT), latent,
        next_latent_sample, sampling_log_probability, advantage,
    )
    down_t, up = pl.pallas_call(
        unpack_kernel,
        out_shape=(
            jax.ShapeDtypeStruct((RANK, DOWN_SHARD), F32),
            jax.ShapeDtypeStruct((RANK, UP_SHARD), F32),
        ),
        in_specs=[vmem],
        out_specs=(vmem, vmem),
        name="unpack",
    )(packed)
    return (down_t.T, up)


def solution(mesh):
    return jax.shard_map(
        body,
        mesh=mesh,
        in_specs=(
            P("group", "tm", "height", None, None),
            P("group", "tm", "height", None, None),
            P("group", "tm", "height", None, None),
            P(),
            P("height", None),
            P(None, "height"),
            P("group", "tm", "height", None, None),
            P("group", None, None),
            P(),
            P(),
            P("group", "tm", "height", None),
            P("group", "tm", "height", None),
            P("group"),
            P("group"),
        ),
        out_specs=(P("height", None), P(None, "height")),
        check_vma=False,
    )
```
